1024 devices in a mesh: dp: 32 (over y, z_lo), rows: 32 (over z_hi, x, core).
Axes of the slice: x: 4, y: 4, z: 32 (z_hi: 4, z_lo: 8; z = z_hi * 8 + z_lo), core: 2. Of those that a mesh axis runs over, the one named last changes fastest.
Arguments:
- images: bfloat16 [32, 256, 64, 384], P('dp', 'rows'), may hold values from -6 to 6
- kernel: float32 [7, 7, 384], replicated, may hold values from -0.875 to 0.875
- conv_bias: float32 [384], replicated, may hold values from -3 to 3
- norm_gain: float32 [384], replicated, may hold values from 0.5 to 1.5
- norm_shift: float32 [384], replicated, may hold values from -3 to 3
- up_weight: bfloat16 [384, 1536], replicated, may hold values from -0.3125 to 0.3125
- up_bias: float32 [1536], replicated, may hold values from -3 to 3
- down_weight: bfloat16 [384, 1536], replicated, may hold values from -0.15625 to 0.15625
- layer_scale: float32 [384], replicated, may hold values from 0.5 to 1.5
- cotangent: bfloat16 [32, 256, 64, 384], P('dp', 'rows'), may hold values from -6 to 6
Outputs:
- grad_images: bfloat16 [32, 256, 64, 384], P('dp', 'rows')
- grad_up: float32 [384, 1536], P('dp', 'rows')
- grad_down: float32 [384, 1536], P('dp', 'rows')
The draws below stay inside these ranges and needn't reach their ends.
All inputs are finite; a program needn't handle non-finite values.
Results may differ from the reference program's by a relative error of at most 0.023.
Values may be sent and summed in bfloat16 or wider, within the bound.
A program may use at most 128 MiB of HBM per device.

```python
import math
import jax
import jax.numpy as jnp
from jax import lax

C = 384
HID = 1536
KS = 7
COLS = 64
BATCH = 32
HEIGHT = 256


def strengthened(drawn, rng, source, target, blocks, factor):
    def block_of(axis_at):
        return (jnp.arange(drawn.shape[axis_at]) // (drawn.shape[axis_at] // blocks)).reshape((-1,) + (1,) * (drawn.ndim - 1 - axis_at))

    first = jax.random.permutation(rng, blocks)[block_of(target)]
    other_side = (block_of(target) + blocks // 2) % blocks
    return jnp.where((block_of(source) == first) | (block_of(source) == other_side), factor * drawn, drawn)


def shard_levels(stream_key, shape, shards, low, high):
    def one(axis_at, blocks):
        steps = jax.random.uniform(jax.random.fold_in(jax.random.fold_in(stream_key, 6), axis_at), (blocks,), jnp.float32, low / len(shards), high / len(shards))
        return jnp.repeat(jnp.exp(steps), shape[axis_at] // blocks).reshape((-1,) + (1,) * (len(shape) - axis_at - 1))

    level = one(*shards[0])
    for cut in shards[1:]:
        level = level * one(*cut)
    return level


def noise(rng, shape, scale, limit, split=(), kind=jnp.bfloat16):
    array = jax.random.normal(rng, shape, jnp.float32) * scale
    if len(split) > 0:
        array = shard_levels(rng, shape, split, -0.22, 0.18) * array
    return jnp.clip(array, min=-limit, max=limit).astype(kind)


def heavy_noise(stream_key, dims, width, limit, cuts, heavy, kind=jnp.bfloat16):
    entries = width * jax.random.normal(stream_key, dims, jnp.float32)
    if cuts:
        entries = entries * shard_levels(stream_key, dims, cuts, -0.22, 0.18)
    return jnp.clip(strengthened(entries, jax.random.fold_in(stream_key, 3), *heavy), -limit, limit).astype(kind)


def setup_inputs(seed: int = 0) -> dict:
    seeds = jax.random.split(jax.random.key(seed), 11)
    return {
        "images": noise(seeds[0], (BATCH, HEIGHT, COLS, C), 1.0, 6.0, ((0, 32), (1, 32))),
        "kernel": noise(seeds[1], (KS, KS, C), (KS * KS) ** -0.5, 0.875, (), jnp.float32),
        "conv_bias": noise(seeds[2], (C,), 0.5, 3.0, (), jnp.float32),
        "norm_gain": jnp.clip(jax.random.uniform(seeds[3], (C,), jnp.float32, 0.5, 1.5), 0.5, 1.5),
        "norm_shift": noise(seeds[4], (C,), 0.5, 3.0, (), jnp.float32),
        "up_weight": noise(seeds[5], (C, HID), C ** -0.5, 0.3125),
        "up_bias": noise(seeds[6], (HID,), 0.5, 3.0, (), jnp.float32),
        "down_weight": noise(seeds[7], (C, HID), HID ** -0.5, 0.15625),
        "layer_scale": jnp.clip(jax.random.uniform(seeds[8], (C,), jnp.float32, 0.5, 1.5), 0.5, 1.5),
        "cotangent": heavy_noise(seeds[9], (BATCH, HEIGHT, COLS, C), 1.0, 6.0, ((0, 32), (1, 32)), (0, 3, 32, 2.75)),
    }


EPSILON = 1e-06

def depthwise(padded, kernel):
    return lax.conv_general_dilated(padded, kernel[:, :, None, :], (1, 1), 'VALID', dimension_numbers=('NHWC', 'HWIO', 'NHWC'), feature_group_count=kernel.shape[2], precision=lax.Precision.HIGHEST)

def gelu_slope(values):
    normal_cdf = 0.5 * (1.0 + jax.scipy.special.erf(values * (1.0 / math.sqrt(2.0))))
    density = jnp.exp(-0.5 * values * values) * (1.0 / math.sqrt(2.0 * math.pi))
    return normal_cdf + values * density

def block_terms(conv_out, norm_gain, norm_shift, up_weight, up_bias, down_weight, layer_scale, cotangent):
    row_mean = lax.optimization_barrier(jnp.mean(conv_out, axis=1, keepdims=True))
    centered = conv_out - row_mean
    inverse = lax.rsqrt(lax.optimization_barrier(jnp.mean(centered * centered, axis=1, keepdims=True)) + EPSILON)
    standard = centered * inverse
    normed = (standard * norm_gain + norm_shift).astype(jnp.bfloat16)
    before = jnp.dot(normed, up_weight, preferred_element_type=jnp.float32) + up_bias
    activated = jax.nn.gelu(before, approximate=False).astype(jnp.bfloat16)
    scaled = (cotangent.astype(jnp.float32) * layer_scale).astype(jnp.bfloat16)
    grad_act = jnp.dot(scaled, down_weight, preferred_element_type=jnp.float32)
    term_down = lax.dot_general(scaled, activated, (((0,), (0,)), ((), ())), preferred_element_type=jnp.float32)
    grad_before = (grad_act * gelu_slope(before)).astype(jnp.bfloat16)
    term_up = lax.dot_general(normed, grad_before, (((0,), (0,)), ((), ())), preferred_element_type=jnp.float32)
    grad_normed = lax.dot_general(grad_before, up_weight, (((1,), (1,)), ((), ())), preferred_element_type=jnp.float32)
    gscaled = grad_normed * norm_gain
    grad_conv = inverse * (gscaled - lax.optimization_barrier(jnp.mean(gscaled, axis=1, keepdims=True)) - standard * lax.optimization_barrier(jnp.mean(gscaled * standard, axis=1, keepdims=True)))
    return (grad_conv.astype(jnp.bfloat16), term_up, term_down)

def reference(images, kernel, conv_bias, norm_gain, norm_shift, up_weight, up_bias, down_weight, layer_scale, cotangent):
    reach = KS // 2
    widths = ((0, 0), (reach, reach), (reach, reach), (0, 0))

    def image_step(totals, pair):
        picture, cot_image = pair
        shape = picture.shape
        padded = jnp.pad(picture.astype(jnp.float32)[None], widths)
        conv_out = depthwise(padded, kernel)[0] + conv_bias
        grad_conv, term_up, term_down = block_terms(conv_out.reshape(-1, shape[2]), norm_gain, norm_shift, up_weight, up_bias, down_weight, layer_scale, cot_image.reshape(-1, shape[2]))
        grad_pad = jnp.pad(grad_conv.reshape(shape).astype(jnp.float32)[None], widths)
        back = depthwise(grad_pad, kernel[::-1, ::-1])[0]
        grad_picture = (cot_image.astype(jnp.float32) + back).astype(jnp.bfloat16)
        return ((totals[0] + term_up, totals[1] + term_down), grad_picture)
    zeros = jnp.zeros((C, HID), jnp.float32)
    totals, grad_images = lax.scan(image_step, (zeros, zeros), (images, cotangent))
    factor = 1.0 / math.sqrt(BATCH * HEIGHT * COLS)
    return (grad_images, totals[0] * factor, totals[1] * factor)
```

```python
import functools
import math

import jax
import jax.numpy as jnp
from jax import lax
from jax.experimental import pallas as pl
from jax.experimental.pallas import tpu as pltpu
from jax.sharding import PartitionSpec as P

EPSILON = 1e-06
MESH = pl.DeviceIdType.MESH
F32 = jnp.float32
BF16 = jnp.bfloat16

NZH, NX, NC, NY, NZL = 4, 4, 2, 4, 8
HB, CB = 48, 12


def extended_2(cells, sides, width):
    for axis, dim in sides:
        count = lax.axis_size(axis)
        ends = count - 1
        head = lax.slice_in_dim(cells, 0, width, axis=dim)
        tail = lax.slice_in_dim(cells, cells.shape[dim] - width, cells.shape[dim], axis=dim)
        cells = jnp.concatenate(
            [
                lax.ppermute(tail, axis, [(i, (i + 1) % count) for i in range(ends)]),
                cells,
                lax.ppermute(head, axis, [((i + 1) % count, i) for i in range(ends)]),
            ],
            axis=dim,
        )
    return cells


def depthwise(padded, kernel):
    return lax.conv_general_dilated(
        padded,
        kernel[:, :, None, :],
        (1, 1),
        "VALID",
        dimension_numbers=("NHWC", "HWIO", "NHWC"),
        feature_group_count=kernel.shape[2],
        precision=lax.Precision.HIGHEST,
    )


def gelu_slope(values):
    normal_cdf = 0.5 * (1.0 + jax.scipy.special.erf(values * (1.0 / math.sqrt(2.0))))
    density = jnp.exp(-0.5 * values * values) * (1.0 / math.sqrt(2.0 * math.pi))
    return normal_cdf + values * density


def coordinates():
    dp, rows = lax.axis_index("dp"), lax.axis_index("rows")
    core, chip = lax.rem(rows, NC), lax.div(rows, NC)
    return (
        lax.div(chip, NX),
        lax.rem(chip, NX),
        core,
        lax.div(dp, NZL),
        lax.rem(dp, NZL),
    )


def device(zh, x, c, y, zl):
    return (y * NZL + zl, (zh * NX + x) * NC + c)


def around(place, step, count):
    return lax.rem(place + step, count)


class Peers:
    def __init__(self):
        self.at = coordinates()

    def core(self):
        zh, x, c, y, zl = self.at
        return device(zh, x, 1 - c, y, zl)

    def x(self, k):
        zh, x, c, y, zl = self.at
        to = around(x, k, NX)
        return to, device(zh, to, c, y, zl)

    def y(self, k):
        zh, x, c, y, zl = self.at
        to = around(y, k, NY)
        return to, device(zh, x, c, to, zl)

    def zl(self, k):
        zh, x, c, y, zl = self.at
        to = around(zl, k, NZL)
        return to, device(zh, x, c, y, to)

    def zh(self, k):
        zh, x, c, y, zl = self.at
        to = around(zh, k, NZH)
        return to, device(to, x, c, y, zl)

    def all(self):
        found = [self.core()]
        for way, count in ((self.x, NX), (self.y, NY), (self.zl, NZL), (self.zh, NZH)):
            found += [way(k)[1] for k in range(1, count)]
        return found


def greet(others):
    barrier = pltpu.get_barrier_semaphore()
    for other in others:
        pl.semaphore_signal(barrier, inc=1, device_id=other, device_id_type=MESH)
    pl.semaphore_wait(barrier, len(others))


def send(src, dst, send_sem, recv_sem, to):
    return pltpu.make_async_remote_copy(
        src_ref=src, dst_ref=dst, send_sem=send_sem, recv_sem=recv_sem, device_id=to, device_id_type=MESH
    )


def spread_channels(values):
    width = NZL * CB
    rows = lax.broadcasted_iota(jnp.int32, (NY * width, NY * 128), 0)
    cols = lax.broadcasted_iota(jnp.int32, (NY * width, NY * 128), 1)
    block, lane = cols // 128, cols % 128
    chosen = jnp.where((lane < width) & (rows == block * width + lane), 1.0, 0.0).astype(BF16)
    return jnp.dot(values, chosen, preferred_element_type=F32).astype(BF16)


def reduce_scratch():
    lanes = NY * 128
    return dict(
        own=pltpu.VMEM((2, NZH, NX, HB, lanes), F32),
        b1=pltpu.VMEM((2, NZH, NX, HB, lanes), BF16),
        r1=pltpu.VMEM((2, NZH, NX, HB, lanes), BF16),
        b2d=pltpu.VMEM((NX, NZH, HB, lanes), BF16),
        r2d=pltpu.VMEM((NX - 1, NZH, HB, lanes), BF16),
        b2u=pltpu.VMEM((NY, NZH, NX, HB, 128), BF16),
        r2u=pltpu.VMEM((NY - 1, NZH, NX, HB, 128), BF16),
        a3u=pltpu.VMEM((NX, NZH, HB, 128), F32),
        b3d=pltpu.VMEM((NY, NZH, HB, 128), BF16),
        r3d=pltpu.VMEM((NY - 1, NZH, HB, 128), BF16),
        b3u=pltpu.VMEM((NX, NZH, HB, 128), BF16),
        r3u=pltpu.VMEM((NX - 1, NZH, HB, 128), BF16),
        b4=pltpu.VMEM((NZL, NZH, 16, 128), BF16),
        r4=pltpu.VMEM((NZL - 1, NZH, 16, 128), BF16),
        a5=pltpu.VMEM((NZH, 16, 128), F32),
        b5=pltpu.VMEM((NZH, 16, 128), BF16),
        r5=pltpu.VMEM((NZH - 1, 16, 128), BF16),
        s1=pltpu.SemaphoreType.DMA((2, 2, NZH)),
        s2d=pltpu.SemaphoreType.DMA((2, NX - 1, NZH)),
        s2u=pltpu.SemaphoreType.DMA((2, NY - 1, NZH)),
        s3d=pltpu.SemaphoreType.DMA((2, NY - 1)),
        s3u=pltpu.SemaphoreType.DMA((2, NX - 1)),
        s4=pltpu.SemaphoreType.DMA((2, NZL - 1)),
        s5=pltpu.SemaphoreType.DMA((2, NZH - 1)),
    )


DOWN, UP = 0, 1


class Reduction:
    def __init__(self, peers, refs):
        self.peers = peers
        self.__dict__.update(refs)

    def first_copy(self, g, z):
        return send(self.b1.at[g, z], self.r1.at[g, z], self.s1.at[0, g, z], self.s1.at[1, g, z], self.peers.core())

    def term(self, g, z, left, right):
        core = self.peers.at[2]
        value = lax.dot_general(left, right, (((0,), (0,)), ((), ())), preferred_element_type=F32)
        value = value.reshape(NX, NC, HB, NY * 128)
        self.own[g, z] = jnp.where(core == 0, value[:, 0], value[:, 1])
        self.b1[g, z] = jnp.where(core == 0, value[:, 1], value[:, 0]).astype(BF16)
        self.first_copy(g, z).start()

    def second_copies(self, g, z):
        p = self.peers
        if g == DOWN:
            for k in range(1, NX):
                to, there = p.x(k)
                yield send(self.b2d.at[to, z], self.r2d.at[k - 1, z], self.s2d.at[0, k - 1, z], self.s2d.at[1, k - 1, z], there)
        else:
            for k in range(1, NY):
                to, there = p.y(k)
                yield send(self.b2u.at[to, z], self.r2u.at[k - 1, z], self.s2u.at[0, k - 1, z], self.s2u.at[1, k - 1, z], there)

    def second(self, g, z):
        self.first_copy(g, z).wait_recv()
        value = self.own[g, z] + self.r1[g, z].astype(F32)
        self.own[g, z] = value
        if g == DOWN:
            for x in range(NX):
                self.b2d[x, z] = value[x].astype(BF16)
        else:
            for y in range(NY):
                self.b2u[y, z] = value[:, :, y * 128 : (y + 1) * 128].astype(BF16)
        for copy in self.second_copies(g, z):
            copy.start()

    def third_copies(self, g):
        p = self.peers
        if g == DOWN:
            for k in range(1, NY):
                to, there = p.y(k)
                yield send(self.b3d.at[to], self.r3d.at[k - 1], self.s3d.at[0, k - 1], self.s3d.at[1, k - 1], there)
        else:
            for k in range(1, NX):
                to, there = p.x(k)
                yield send(self.b3u.at[to], self.r3u.at[k - 1], self.s3u.at[0, k - 1], self.s3u.at[1, k - 1], there)

    def third_sum(self, g, z):
        zh, x, c, y, zl = self.peers.at
        for copy in self.second_copies(g, z):
            copy.wait_recv()
        if g == DOWN:
            value = self.own[g, z, x]
            for k in range(NX - 1):
                value = value + self.r2d[k, z].astype(F32)
            self.own[g, z, x] = value
            for j in range(NY):
                self.b3d[j, z] = value[:, j * 128 : (j + 1) * 128].astype(BF16)
        else:
            value = self.own[g, z, :, :, pl.ds(pl.multiple_of(y * 128, 128), 128)]
            for k in range(NY - 1):
                value = value + self.r2u[k, z].astype(F32)
            for j in range(NX):
                self.a3u[j, z] = value[j]
                self.b3u[j, z] = value[j].astype(BF16)

    def third(self, g):
        @pl.loop(0, NZH)
        def _(z):
            self.third_sum(g, z)

        for copy in self.third_copies(g):
            copy.start()

    def fourth_copies(self):
        for k in range(1, NZL):
            to, there = self.peers.zl(k)
            yield send(self.b4.at[to], self.r4.at[k - 1], self.s4.at[0, k - 1], self.s4.at[1, k - 1], there)

    def fourth(self):
        zh, x, c, y, zl = self.peers.at
        for g in (DOWN, UP):
            for copy in self.third_copies(g):
                copy.wait_recv()
        shape = (NZL * 16, 128)
        rows, cols = lax.broadcasted_iota(jnp.int32, shape, 0), lax.broadcasted_iota(jnp.int32, shape, 1)
        chosen = jnp.where((rows % 16 < CB) & (cols == (rows // 16) * CB + rows % 16), 1.0, 0.0).astype(BF16)

        @pl.loop(0, NZH)
        def _(z):
            up = self.a3u[x, z]
            for k in range(NX - 1):
                up = up + self.r3u[k, z].astype(F32)
            down = self.own[DOWN, z, x, :, pl.ds(pl.multiple_of(y * 128, 128), 128)]
            for k in range(NY - 1):
                down = down + self.r3d[k, z].astype(F32)
            both = jnp.concatenate([up, down, jnp.zeros((128 - 2 * HB, 128), F32)], axis=0).astype(BF16)
            placed = lax.dot_general(chosen, both, (((1,), (1,)), ((), ())), preferred_element_type=F32)
            placed = placed.reshape(NZL, 16, 128).astype(BF16)
            for j in range(NZL):
                self.b4[j, z] = placed[j]

        for copy in self.fourth_copies():
            copy.start()

    def fifth_copies(self):
        for k in range(1, NZH):
            to, there = self.peers.zh(k)
            yield send(self.b5.at[to], self.r5.at[k - 1], self.s5.at[0, k - 1], self.s5.at[1, k - 1], there)

    def fifth(self):
        zl = self.peers.at[4]
        value = self.b4[zl].astype(F32)
        for k, copy in enumerate(self.fourth_copies()):
            copy.wait_recv()
            value = value + self.r4[k].astype(F32)
        self.a5[...] = value
        self.b5[...] = value.astype(BF16)
        for copy in self.fifth_copies():
            copy.start()

    def finish(self, factor, up_ref, down_ref):
        zh = self.peers.at[0]
        value = self.a5[zh]
        for k, copy in enumerate(self.fifth_copies()):
            copy.wait_recv()
            value = value + self.r5[k].astype(F32)
        value = value * factor
        up_ref[...] = value[:CB, :HB]
        down_ref[...] = pltpu.roll(value, 128 - HB, 1)[:CB, :HB]

    def drain(self):
        @pl.loop(0, NZH)
        def _(z):
            for g in (DOWN, UP):
                self.first_copy(g, z).wait_send()
                for copy in self.second_copies(g, z):
                    copy.wait_send()

        for g in (DOWN, UP):
            for copy in self.third_copies(g):
                copy.wait_send()
        for copy in self.fourth_copies():
            copy.wait_send()
        for copy in self.fifth_copies():
            copy.wait_send()


def sums_kernel(factor, names, scaled_ref, activated_ref, normed_ref, slope_ref, up_ref, down_ref, *scratch):
    peers = Peers()
    sums = Reduction(peers, dict(zip(names, scratch)))
    greet(peers.all())
    rows = NX * NC * HB
    for g, left_ref, right_ref in ((DOWN, activated_ref, scaled_ref), (UP, slope_ref, normed_ref)):
        right = spread_channels(right_ref[...])

        @pl.loop(0, NZH)
        def _(z, g=g, left_ref=left_ref, right=right):
            sums.term(g, z, left_ref[:, pl.ds(pl.multiple_of(z * rows, rows), rows)], right)

    for g in (DOWN, UP):

        @pl.loop(0, NZH)
        def _(z, g=g):
            sums.second(g, z)

    for g in (DOWN, UP):
        sums.third(g)
    sums.fourth()
    sums.fifth()
    sums.finish(factor, up_ref, down_ref)
    sums.drain()


def weight_sums(factor, scaled, activated, normed, grad_before):
    scratch = reduce_scratch()
    block = jax.ShapeDtypeStruct((CB, HB), F32)
    vmem = pl.BlockSpec(memory_space=pltpu.VMEM)
    return pl.pallas_call(
        functools.partial(sums_kernel, factor, tuple(scratch)),
        out_shape=(block, block),
        in_specs=[vmem] * 4,
        out_specs=(vmem, vmem),
        scratch_shapes=list(scratch.values()),
        compiler_params=pltpu.CompilerParams(
            collective_id=0, has_side_effects=True, vmem_limit_bytes=48 * 1024 * 1024
        ),
    )(scaled, activated, normed, grad_before)


def block_terms(
    conv_out, norm_gain, norm_shift, up_weight, up_bias, down_weight, layer_scale, cotangent
):
    row_mean = jnp.mean(conv_out, axis=1, keepdims=True)
    centered = conv_out - row_mean
    inverse = lax.rsqrt(jnp.mean(centered * centered, axis=1, keepdims=True) + EPSILON)
    standard = centered * inverse
    normed = (standard * norm_gain + norm_shift).astype(jnp.bfloat16)
    before = jnp.dot(normed, up_weight, preferred_element_type=jnp.float32) + up_bias
    activated = jax.nn.gelu(before, approximate=False).astype(jnp.bfloat16)
    scaled = (cotangent.astype(jnp.float32) * layer_scale).astype(jnp.bfloat16)
    grad_act = jnp.dot(scaled, down_weight, preferred_element_type=jnp.float32)
    grad_before = (grad_act * gelu_slope(before)).astype(jnp.bfloat16)
    grad_normed = lax.dot_general(
        grad_before, up_weight, (((1,), (1,)), ((), ())), preferred_element_type=jnp.float32
    )
    gscaled = grad_normed * norm_gain
    grad_conv = inverse * (
        gscaled
        - jnp.mean(gscaled, axis=1, keepdims=True)
        - standard * jnp.mean(gscaled * standard, axis=1, keepdims=True)
    )
    return (grad_conv.astype(jnp.bfloat16), scaled, activated, normed, grad_before)


def on_device(
    images,
    kernel,
    conv_bias,
    norm_gain,
    norm_shift,
    up_weight,
    up_bias,
    down_weight,
    layer_scale,
    cotangent,
):
    reach = kernel.shape[0] // 2
    shape = images.shape
    channels = shape[3]
    side_pad = ((0, 0), (0, 0), (reach, reach), (0, 0))
    extended = extended_2(images, (("rows", 1),), reach)
    padded = jnp.pad(extended.astype(jnp.float32), side_pad)
    conv_out = depthwise(padded, kernel) + conv_bias
    grad_conv, scaled, activated, normed, grad_before = block_terms(
        conv_out.reshape(-1, channels),
        norm_gain,
        norm_shift,
        up_weight,
        up_bias,
        down_weight,
        layer_scale,
        cotangent.reshape(-1, channels),
    )
    grad_ext = extended_2(grad_conv.reshape(shape), (("rows", 1),), reach)
    grad_pad = jnp.pad(grad_ext.astype(jnp.float32), side_pad)
    back = depthwise(grad_pad, kernel[::-1, ::-1])
    grad_images = (cotangent.astype(jnp.float32) + back).astype(jnp.bfloat16)
    groups = lax.axis_size("dp")
    parts = lax.axis_size("rows")
    factor = 1.0 / math.sqrt(shape[0] * shape[1] * shape[2] * groups * parts)
    grad_up, grad_down = weight_sums(factor, scaled, activated, normed, grad_before)
    return (grad_images, grad_up, grad_down)


def solution(mesh):
    in_specs = (
        P("dp", "rows", None, None),
        P(),
        P(),
        P(),
        P(),
        P(),
        P(),
        P(),
        P(),
        P("dp", "rows", None, None),
    )
    out_specs = (P("dp", "rows", None, None), P("dp", "rows"), P("dp", "rows"))
    return jax.shard_map(
        on_device, mesh=mesh, in_specs=in_specs, out_specs=out_specs, check_vma=False
    )
```

```python
import functools
import math

import jax
import jax.numpy as jnp
from jax import lax
from jax.experimental import pallas as pl
from jax.experimental.pallas import tpu as pltpu
from jax.sharding import PartitionSpec as P

EPSILON = 1e-06
MESH = pl.DeviceIdType.MESH
F32 = jnp.float32
BF16 = jnp.bfloat16

NZH, NX, NC, NY, NZL = 4, 4, 2, 4, 8
NROWS = NZH * NX * NC
HB, CB = 48, 12


def coordinates():
    dp, rows = lax.axis_index("dp"), lax.axis_index("rows")
    core, chip = lax.rem(rows, NC), lax.div(rows, NC)
    return (
        lax.div(chip, NX),
        lax.rem(chip, NX),
        core,
        lax.div(dp, NZL),
        lax.rem(dp, NZL),
    )


def device(zh, x, c, y, zl):
    return (y * NZL + zl, (zh * NX + x) * NC + c)


def around(place, step, count):
    return lax.rem(place + step, count)


class Peers:
    def __init__(self):
        self.at = coordinates()

    def core(self):
        zh, x, c, y, zl = self.at
        return device(zh, x, 1 - c, y, zl)

    def x(self, k):
        zh, x, c, y, zl = self.at
        to = around(x, k, NX)
        return to, device(zh, to, c, y, zl)

    def y(self, k):
        zh, x, c, y, zl = self.at
        to = around(y, k, NY)
        return to, device(zh, x, c, to, zl)

    def zl(self, k):
        zh, x, c, y, zl = self.at
        to = around(zl, k, NZL)
        return to, device(zh, x, c, y, to)

    def zh(self, k):
        zh, x, c, y, zl = self.at
        to = zh + 1 - 2 * lax.rem(zh, 2) if k == 0 else NZH - 1 - zh
        return to, device(to, x, c, y, zl)

    def strip(self, step):
        zh, x, c, y, zl = self.at
        row = around((zh * NX + x) * NC + c, step + NROWS, NROWS)
        return (y * NZL + zl, row)

    def all(self):
        found = [self.core(), self.strip(-1), self.strip(1), self.zh(0)[1], self.zh(1)[1]]
        for way, count in ((self.x, NX), (self.y, NY), (self.zl, NZL)):
            found += [way(k)[1] for k in range(1, count)]
        return found


def greet(others):
    barrier = pltpu.get_barrier_semaphore()
    for other in others:
        pl.semaphore_signal(barrier, inc=1, device_id=other, device_id_type=MESH)


def await_greetings(others):
    pl.semaphore_wait(pltpu.get_barrier_semaphore(), len(others))


def send(src, dst, send_sem, recv_sem, to):
    return pltpu.make_async_remote_copy(
        src_ref=src, dst_ref=dst, send_sem=send_sem, recv_sem=recv_sem, device_id=to, device_id_type=MESH
    )


def spread_channels(values):
    width = NZL * CB
    rows = lax.broadcasted_iota(jnp.int32, (NY * width, NY * 128), 0)
    cols = lax.broadcasted_iota(jnp.int32, (NY * width, NY * 128), 1)
    block, lane = cols // 128, cols % 128
    chosen = jnp.where((lane < width) & (rows == block * width + lane), 1.0, 0.0).astype(BF16)
    return jnp.dot(values, chosen, preferred_element_type=F32).astype(BF16)


def reduce_scratch():
    lanes = NY * 128
    return dict(
        own=pltpu.VMEM((2, NZH, NX, HB, lanes), F32),
        b1=pltpu.VMEM((2, NZH, NX, HB, lanes), BF16),
        r1=pltpu.VMEM((2, NZH, NX, HB, lanes), BF16),
        b2d=pltpu.VMEM((NX, NZH, HB, lanes), BF16),
        r2d=pltpu.VMEM((NX - 1, NZH, HB, lanes), BF16),
        b2u=pltpu.VMEM((NY, NZH, NX, HB, 128), BF16),
        r2u=pltpu.VMEM((NY - 1, NZH, NX, HB, 128), BF16),
        a3u=pltpu.VMEM((NX, NZH, HB, 128), F32),
        b3d=pltpu.VMEM((NY, NZH, HB, 128), BF16),
        r3d=pltpu.VMEM((NY - 1, NZH, HB, 128), BF16),
        b3u=pltpu.VMEM((NX, NZH, HB, 128), BF16),
        r3u=pltpu.VMEM((NX - 1, NZH, HB, 128), BF16),
        b4=pltpu.VMEM((NZL, NZH, 16, 128), BF16),
        r4=pltpu.VMEM((NZL - 1, NZH, 16, 128), BF16),
        a5=pltpu.VMEM((NZH, 16, 128), F32),
        b5=pltpu.VMEM((NZH, 16, 128), BF16),
        b6=pltpu.VMEM((16, 128), BF16),
        r5=pltpu.VMEM((3, 16, 128), BF16),
        total=pltpu.VMEM((2, NZH, NX * NC * HB, lanes), F32),
        s1=pltpu.SemaphoreType.DMA((2, 2, NZH)),
        s2d=pltpu.SemaphoreType.DMA((2, NX - 1, NZH)),
        s2u=pltpu.SemaphoreType.DMA((2, NY - 1, NZH)),
        s3d=pltpu.SemaphoreType.DMA((2, NY - 1)),
        s3u=pltpu.SemaphoreType.DMA((2, NX - 1)),
        s4=pltpu.SemaphoreType.DMA((2, NZL - 1)),
        s5=pltpu.SemaphoreType.DMA((2, 3)),
    )


DOWN, UP = 0, 1


class Reduction:
    def __init__(self, peers, refs):
        self.peers = peers
        self.__dict__.update(refs)

    def first_copy(self, g, z):
        return send(self.b1.at[g, z], self.r1.at[g, z], self.s1.at[0, g, z], self.s1.at[1, g, z], self.peers.core())

    def term(self, g, z, left, right, last):
        core = self.peers.at[2]
        value = lax.dot_general(left, right, (((0,), (0,)), ((), ())), preferred_element_type=F32)

        @pl.when(jnp.logical_not(last))
        def _():
            self.total[g, z] = value

        @pl.when(last)
        def _():
            whole = (value + self.total[g, z]).reshape(NX, NC, HB, NY * 128)
            self.own[g, z] = jnp.where(core == 0, whole[:, 0], whole[:, 1])
            self.b1[g, z] = jnp.where(core == 0, whole[:, 1], whole[:, 0]).astype(BF16)
            self.first_copy(g, z).start()

    def second_copies(self, g, z):
        p = self.peers
        if g == DOWN:
            for k in range(1, NX):
                to, there = p.x(k)
                yield send(self.b2d.at[to, z], self.r2d.at[k - 1, z], self.s2d.at[0, k - 1, z], self.s2d.at[1, k - 1, z], there)
        else:
            for k in range(1, NY):
                to, there = p.y(k)
                yield send(self.b2u.at[to, z], self.r2u.at[k - 1, z], self.s2u.at[0, k - 1, z], self.s2u.at[1, k - 1, z], there)

    def second(self, g, z):
        self.first_copy(g, z).wait_recv()
        value = self.own[g, z] + self.r1[g, z].astype(F32)
        self.own[g, z] = value
        if g == DOWN:
            for x in range(NX):
                self.b2d[x, z] = value[x].astype(BF16)
        else:
            for y in range(NY):
                self.b2u[y, z] = value[:, :, y * 128 : (y + 1) * 128].astype(BF16)
        for copy in self.second_copies(g, z):
            copy.start()

    def third_copies(self, g):
        p = self.peers
        if g == DOWN:
            for k in range(1, NY):
                to, there = p.y(k)
                yield send(self.b3d.at[to], self.r3d.at[k - 1], self.s3d.at[0, k - 1], self.s3d.at[1, k - 1], there)
        else:
            for k in range(1, NX):
                to, there = p.x(k)
                yield send(self.b3u.at[to], self.r3u.at[k - 1], self.s3u.at[0, k - 1], self.s3u.at[1, k - 1], there)

    def third_sum(self, g, z):
        zh, x, c, y, zl = self.peers.at
        for copy in self.second_copies(g, z):
            copy.wait_recv()
        if g == DOWN:
            value = self.own[g, z, x]
            for k in range(NX - 1):
                value = value + self.r2d[k, z].astype(F32)
            self.own[g, z, x] = value
            for j in range(NY):
                self.b3d[j, z] = value[:, j * 128 : (j + 1) * 128].astype(BF16)
        else:
            value = self.own[g, z, :, :, pl.ds(pl.multiple_of(y * 128, 128), 128)]
            for k in range(NY - 1):
                value = value + self.r2u[k, z].astype(F32)
            for j in range(NX):
                self.a3u[j, z] = value[j]
                self.b3u[j, z] = value[j].astype(BF16)

    def third(self, g):
        @pl.loop(0, NZH)
        def _(z):
            self.third_sum(g, z)

        for copy in self.third_copies(g):
            copy.start()

    def fourth_copies(self):
        for k in range(1, NZL):
            to, there = self.peers.zl(k)
            yield send(self.b4.at[to], self.r4.at[k - 1], self.s4.at[0, k - 1], self.s4.at[1, k - 1], there)

    def fourth(self):
        zh, x, c, y, zl = self.peers.at
        for g in (DOWN, UP):
            for copy in self.third_copies(g):
                copy.wait_recv()
        shape = (NZL * 16, 128)
        rows, cols = lax.broadcasted_iota(jnp.int32, shape, 0), lax.broadcasted_iota(jnp.int32, shape, 1)
        chosen = jnp.where((rows % 16 < CB) & (cols == (rows // 16) * CB + rows % 16), 1.0, 0.0).astype(BF16)

        @pl.loop(0, NZH)
        def _(z):
            up = self.a3u[x, z]
            for k in range(NX - 1):
                up = up + self.r3u[k, z].astype(F32)
            down = self.own[DOWN, z, x, :, pl.ds(pl.multiple_of(y * 128, 128), 128)]
            for k in range(NY - 1):
                down = down + self.r3d[k, z].astype(F32)
            both = jnp.concatenate([up, down, jnp.zeros((128 - 2 * HB, 128), F32)], axis=0).astype(BF16)
            placed = lax.dot_general(chosen, both, (((1,), (1,)), ((), ())), preferred_element_type=F32)
            placed = placed.reshape(NZL, 16, 128).astype(BF16)
            for j in range(NZL):
                self.b4[j, z] = placed[j]

        for copy in self.fourth_copies():
            copy.start()

    def fifth_copies(self):
        to, there = self.peers.zh(0)
        for k, block in enumerate((to, NZH - 1 - to)):
            yield send(self.b5.at[block], self.r5.at[k], self.s5.at[0, k], self.s5.at[1, k], there)

    def sixth_copy(self):
        to, there = self.peers.zh(1)
        return send(self.b6, self.r5.at[2], self.s5.at[0, 2], self.s5.at[1, 2], there)

    def fifth(self):
        zl = self.peers.at[4]
        value = self.b4[zl].astype(F32)
        for k, copy in enumerate(self.fourth_copies()):
            copy.wait_recv()
            value = value + self.r4[k].astype(F32)
        self.a5[...] = value
        self.b5[...] = value.astype(BF16)
        for copy in self.fifth_copies():
            copy.start()

    def sixth(self):
        zh = self.peers.at[0]
        for copy in self.fifth_copies():
            copy.wait_recv()
        self.b6[...] = (self.a5[NZH - 1 - zh] + self.r5[1].astype(F32)).astype(BF16)
        self.sixth_copy().start()

    def finish(self, factor, up_ref, down_ref):
        zh = self.peers.at[0]
        value = self.a5[zh] + self.r5[0].astype(F32)
        self.sixth_copy().wait_recv()
        value = (value + self.r5[2].astype(F32)) * factor
        up_ref[...] = value[:CB, :HB]
        down_ref[...] = pltpu.roll(value, 128 - HB, 1)[:CB, :HB]

    def drain(self):
        @pl.loop(0, NZH)
        def _(z):
            for g in (DOWN, UP):
                self.first_copy(g, z).wait_send()
                for copy in self.second_copies(g, z):
                    copy.wait_send()

        for g in (DOWN, UP):
            for copy in self.third_copies(g):
                copy.wait_send()
        for copy in self.fourth_copies():
            copy.wait_send()
        for copy in self.fifth_copies():
            copy.wait_send()
        self.sixth_copy().wait_send()


KS, REACH = 7, 3
HROWS, COLS = 8, 64
HALF = HROWS // 2 * COLS


def row_sum(rows, kernel_ref, lanes, flip):
    col = lax.broadcasted_iota(jnp.int32, (COLS, 128), 0)
    total = None
    for j in range(KS):
        part = None
        for value, i in rows:
            a, b = (KS - 1 - i, KS - 1 - j) if flip else (i, j)
            tap = value * kernel_ref[a, b : b + 1, lanes]
            part = tap if part is None else part + tap
        shift = j - REACH
        if shift != 0:
            inside = (col + shift >= 0) & (col + shift < COLS)
            part = jnp.where(inside, pltpu.roll(part, (-shift) % COLS, 0), 0.0)
        total = part if total is None else total + part
    return total


def own_rows(source, sums, kernel_ref, flip):
    @pl.loop(0, source.shape[2] // 128)
    def _(block):
        lanes = pl.ds(pl.multiple_of(block * 128, 128), 128)

        @pl.loop(0, HROWS)
        def _(h):
            rows = [(source[h + i, :, lanes], i) for i in range(KS)]
            sums[h, :, lanes] = row_sum(rows, kernel_ref, lanes, flip)


def halo_rows(halo, side, sums, kernel_ref, flip):
    for static_side in (0, 1):

        @pl.when(side == static_side)
        def _(static_side=static_side):
            @pl.loop(0, sums.shape[2] // 128)
            def _(block):
                lanes = pl.ds(pl.multiple_of(block * 128, 128), 128)
                rows = [halo[static_side, r * COLS : (r + 1) * COLS, lanes].astype(F32) for r in range(REACH)]
                for h in range(REACH):
                    if static_side == 0:
                        used, at = [(rows[r], r - h) for r in range(h, REACH)], h
                    else:
                        used, at = [(rows[r], KS - 1 + r - h) for r in range(h + 1)], HROWS - REACH + h
                    sums[at, :, lanes] = sums[at, :, lanes] + row_sum(used, kernel_ref, lanes, flip)


def gelu_parts(values):
    denominator = 1.0 + 0.2316419 * jnp.abs(values)
    guess = pl.reciprocal(denominator, approx=True)
    t = guess * (2.0 - denominator * guess)
    density = jnp.exp2(values * values * (-0.5 * math.log2(math.e))) * (1.0 / math.sqrt(2.0 * math.pi))
    series = t * (0.319381530 + t * (-0.356563782 + t * (1.781477937 + t * (-1.821255978 + t * 1.330274429))))
    tail = density * series
    cdf = jnp.where(values >= 0.0, 1.0 - tail, tail)
    return values * cdf, cdf + values * density


def block_kernel(factor, names, images, kernel, conv_bias, gain, shift, up_weight, up_bias, down_weight, scale, cotangent,
                 out, up_out, down_out, *scratch):
    s = dict(zip(names, scratch))
    peers = Peers()
    others = peers.all()
    greet(others)
    sums = Reduction(peers, s)
    zh, x, c, y, zl = peers.at
    strip = (zh * NX + x) * NC + c
    channels, hidden = up_weight.shape
    width = NX * NC * HB
    source, gradient, conv = s["source"], s["gradient"], s["conv"]
    scaled, spread_scaled, grad_act = s["scaled"], s["spread_scaled"], s["grad_act"]
    standard, inverse, normed, spread_normed = s["standard"], s["inverse"], s["normed"], s["spread_normed"]
    before, activated, slope, grad_normed, grad_conv = s["before"], s["activated"], s["slope"], s["grad_normed"], s["grad_conv"]

    def chunk(n):
        return pl.ds(pl.multiple_of(n * width, 128), width)

    def has_neighbour(side):
        return jnp.where(side == 0, strip > 0, strip < NROWS - 1)

    def halo_copy(strip_ref, halo, sems, side):
        first = pl.multiple_of(side * ((HROWS - REACH) * COLS), COLS)
        return send(strip_ref.at[pl.ds(first, REACH * COLS)], halo.at[1 - side], sems.at[0, side], sems.at[1, 1 - side],
                    peers.strip(2 * side - 1))

    def arrived(strip_ref, halo, sems, side):
        halo_copy(strip_ref, halo, sems, 1 - side).wait_recv()

    for rows in (source, gradient):
        rows[:REACH] = jnp.zeros((REACH, COLS, channels), F32)
        rows[REACH + HROWS :] = jnp.zeros((REACH, COLS, channels), F32)

    @pl.loop(0, HROWS)
    def _(h):
        at = pl.ds(pl.multiple_of(h * COLS, COLS), COLS)
        source[REACH + h] = images[at, :].astype(F32)
        scaled[at, :] = (cotangent[at, :].astype(F32) * scale[...]).astype(BF16)

    own_rows(source, conv, kernel, False)
    spread_scaled[...] = spread_channels(scaled[...])

    @pl.loop(0, NZH)
    def _(n):
        grad_act[:, chunk(n)] = jnp.dot(scaled[...], down_weight[:, chunk(n)], preferred_element_type=F32)

    await_greetings(others)
    for side in (0, 1):

        @pl.when(has_neighbour(side))
        def _(side=side):
            halo_copy(images, s["image_halo"], s["image_sems"], side).start()

    early = jnp.where((x == 0) & (c == 0), 1, 0)

    @pl.loop(0, 2)
    def _(step):
        half = jnp.where(step == 0, early, 1 - early)
        last = step == 1

        @pl.when(has_neighbour(half))
        def _():
            arrived(images, s["image_halo"], s["image_sems"], half)
            halo_rows(s["image_halo"], half, conv, kernel, False)

        pixels = pl.ds(pl.multiple_of(half * HALF, HALF), HALF)

        @pl.loop(0, HROWS // 2)
        def _(k):
            h = half * (HROWS // 2) + k
            at = pl.ds(pl.multiple_of(h * COLS, COLS), COLS)
            value = conv[h] + conv_bias[...]
            centered = value - jnp.sum(value, axis=1, keepdims=True) * (1.0 / channels)
            inv = lax.rsqrt(jnp.sum(centered * centered, axis=1, keepdims=True) * (1.0 / channels) + EPSILON)
            std = centered * inv
            standard[at, :] = std
            inverse[at, :] = inv
            normed[at, :] = (std * gain[...] + shift[...]).astype(BF16)

        spread_normed[...] = spread_channels(normed[pixels, :])

        @pl.loop(0, NZH)
        def _(n):
            weights = up_weight[:, chunk(n)]
            before[...] = jnp.dot(normed[pixels, :], weights, preferred_element_type=F32)

            @pl.loop(0, HALF // TILE)
            def _(k):
                at = pl.ds(pl.multiple_of(k * TILE, TILE), TILE)
                act, slopes = gelu_parts(before[at, :] + up_bias[:, chunk(n)])
                activated[at, :] = act.astype(BF16)
                grads = grad_act[pl.ds(pl.multiple_of(half * HALF + k * TILE, TILE), TILE), chunk(n)]
                slope[at, :] = (grads * slopes).astype(BF16)

            sums.term(DOWN, n, activated[...], spread_scaled[pixels, :], last)
            sums.term(UP, n, slope[...], spread_normed[...], last)
            back = lax.dot_general(slope[...], weights, (((1,), (1,)), ((), ())), preferred_element_type=F32)

            @pl.when(n == 0)
            def _():
                grad_normed[...] = back

            @pl.when(n > 0)
            def _():
                grad_normed[...] = grad_normed[...] + back

            @pl.when(last & (n > 0))
            def _():
                sums.second(DOWN, n - 1)
                sums.second(UP, n - 1)

        @pl.loop(0, HROWS // 2)
        def _(k):
            h = half * (HROWS // 2) + k
            at = pl.ds(pl.multiple_of(h * COLS, COLS), COLS)
            gscaled = grad_normed[pl.ds(pl.multiple_of(k * COLS, COLS), COLS), :] * gain[...]
            std = standard[at, :]
            mean = jnp.sum(gscaled, axis=1, keepdims=True) * (1.0 / channels)
            along = jnp.sum(gscaled * std, axis=1, keepdims=True) * (1.0 / channels)
            value = (inverse[at, :] * (gscaled - mean - std * along)).astype(BF16)
            grad_conv[at, :] = value
            gradient[REACH + h] = value.astype(F32)

        @pl.when(has_neighbour(half))
        def _():
            halo_copy(grad_conv, s["grad_halo"], s["grad_sems"], half).start()

    for g in (DOWN, UP):
        sums.second(g, NZH - 1)
    own_rows(gradient, conv, kernel, True)
    for g in (DOWN, UP):
        sums.third(g)
    sums.fourth()
    for step in (0, 1):
        side = jnp.where(step == 0, early, 1 - early)

        @pl.when(has_neighbour(side))
        def _(side=side):
            arrived(grad_conv, s["grad_halo"], s["grad_sems"], side)
            halo_rows(s["grad_halo"], side, conv, kernel, True)

    @pl.loop(0, HROWS)
    def _(h):
        at = pl.ds(pl.multiple_of(h * COLS, COLS), COLS)
        out[at, :] = (cotangent[at, :].astype(F32) + conv[h]).astype(BF16)

    sums.fifth()
    sums.sixth()
    sums.finish(factor, up_out, down_out)
    sums.drain()
    for strip_ref, halo, sems in ((images, s["image_halo"], s["image_sems"]), (grad_conv, s["grad_halo"], s["grad_sems"])):
        for side in (0, 1):

            @pl.when(has_neighbour(side))
            def _(strip_ref=strip_ref, halo=halo, sems=sems, side=side):
                halo_copy(strip_ref, halo, sems, side).wait_send()


TILE = 64


def on_device(
    images,
    kernel,
    conv_bias,
    norm_gain,
    norm_shift,
    up_weight,
    up_bias,
    down_weight,
    layer_scale,
    cotangent,
):
    shape = images.shape
    channels, hidden = up_weight.shape
    pixels = shape[0] * shape[1] * shape[2]
    groups, parts = lax.axis_size("dp"), lax.axis_size("rows")
    factor = 1.0 / math.sqrt(pixels * groups * parts)
    scratch = reduce_scratch() | dict(
        source=pltpu.VMEM((HROWS + 2 * REACH, COLS, channels), F32),
        gradient=pltpu.VMEM((HROWS + 2 * REACH, COLS, channels), F32),
        conv=pltpu.VMEM((HROWS, COLS, channels), F32),
        scaled=pltpu.VMEM((pixels, channels), BF16),
        spread_scaled=pltpu.VMEM((pixels, NY * 128), BF16),
        grad_act=pltpu.VMEM((pixels, hidden), F32),
        standard=pltpu.VMEM((pixels, channels), F32),
        inverse=pltpu.VMEM((pixels, 1), F32),
        normed=pltpu.VMEM((pixels, channels), BF16),
        spread_normed=pltpu.VMEM((HALF, NY * 128), BF16),
        before=pltpu.VMEM((HALF, NX * NC * HB), F32),
        activated=pltpu.VMEM((HALF, NX * NC * HB), BF16),
        slope=pltpu.VMEM((HALF, NX * NC * HB), BF16),
        grad_normed=pltpu.VMEM((HALF, channels), F32),
        grad_conv=pltpu.VMEM((pixels, channels), BF16),
        image_halo=pltpu.VMEM((2, REACH * COLS, channels), BF16),
        grad_halo=pltpu.VMEM((2, REACH * COLS, channels), BF16),
        image_sems=pltpu.SemaphoreType.DMA((2, 2)),
        grad_sems=pltpu.SemaphoreType.DMA((2, 2)),
    )
    block = jax.ShapeDtypeStruct((CB, HB), F32)
    vmem = pl.BlockSpec(memory_space=pltpu.VMEM)
    row = lambda vector: vector.reshape(1, -1)
    grad_images, grad_up, grad_down = pl.pallas_call(
        functools.partial(block_kernel, factor, tuple(scratch)),
        out_shape=(jax.ShapeDtypeStruct((pixels, channels), BF16), block, block),
        in_specs=[vmem] * 10,
        out_specs=(vmem, vmem, vmem),
        scratch_shapes=list(scratch.values()),
        compiler_params=pltpu.CompilerParams(
            collective_id=0, has_side_effects=True, vmem_limit_bytes=56 * 1024 * 1024
        ),
    )(
        images.reshape(pixels, channels),
        kernel,
        row(conv_bias),
        row(norm_gain),
        row(norm_shift),
        up_weight,
        row(up_bias),
        down_weight,
        row(layer_scale),
        cotangent.reshape(pixels, channels),
    )
    return (grad_images.reshape(shape), grad_up, grad_down)


def solution(mesh):
    in_specs = (
        P("dp", "rows", None, None),
        P(),
        P(),
        P(),
        P(),
        P(),
        P(),
        P(),
        P(),
        P("dp", "rows", None, None),
    )
    out_specs = (P("dp", "rows", None, None), P("dp", "rows"), P("dp", "rows"))
    return jax.shard_map(
        on_device, mesh=mesh, in_specs=in_specs, out_specs=out_specs, check_vma=False
    )
```

```python
import functools
import math

import jax
import jax.numpy as jnp
from jax import lax
from jax.experimental import pallas as pl
from jax.experimental.pallas import tpu as pltpu
from jax.sharding import PartitionSpec as P

EPSILON = 1e-06
MESH = pl.DeviceIdType.MESH
F32 = jnp.float32
BF16 = jnp.bfloat16

NZH, NX, NC, NY, NZL = 4, 4, 2, 4, 8
NROWS = NZH * NX * NC
HB, CB = 48, 12


def coordinates():
    dp, rows = lax.axis_index("dp"), lax.axis_index("rows")
    core, chip = lax.rem(rows, NC), lax.div(rows, NC)
    return (
        lax.div(chip, NX),
        lax.rem(chip, NX),
        core,
        lax.div(dp, NZL),
        lax.rem(dp, NZL),
    )


def device(zh, x, c, y, zl):
    return (y * NZL + zl, (zh * NX + x) * NC + c)


def around(place, step, count):
    return lax.rem(place + step, count)


class Peers:
    def __init__(self):
        self.at = coordinates()

    def core(self):
        zh, x, c, y, zl = self.at
        return device(zh, x, 1 - c, y, zl)

    def x(self, k):
        zh, x, c, y, zl = self.at
        to = around(x, k, NX)
        return to, device(zh, to, c, y, zl)

    def y(self, k):
        zh, x, c, y, zl = self.at
        to = around(y, k, NY)
        return to, device(zh, x, c, to, zl)

    def zl(self, k):
        zh, x, c, y, zl = self.at
        to = around(zl, k, NZL)
        return to, device(zh, x, c, y, to)

    def zh(self, k):
        zh, x, c, y, zl = self.at
        to = zh + 1 - 2 * lax.rem(zh, 2) if k == 0 else NZH - 1 - zh
        return to, device(to, x, c, y, zl)

    def strip(self, step):
        zh, x, c, y, zl = self.at
        row = around((zh * NX + x) * NC + c, step + NROWS, NROWS)
        return (y * NZL + zl, row)

    def all(self):
        found = [self.core(), self.strip(-1), self.strip(1), self.zh(0)[1], self.zh(1)[1]]
        for way, count in ((self.x, NX), (self.y, NY), (self.zl, NZL)):
            found += [way(k)[1] for k in range(1, count)]
        return found


def greet(others):
    barrier = pltpu.get_barrier_semaphore()
    for other in others:
        pl.semaphore_signal(barrier, inc=1, device_id=other, device_id_type=MESH)


def await_greetings(others):
    pl.semaphore_wait(pltpu.get_barrier_semaphore(), len(others))


def send(src, dst, send_sem, recv_sem, to):
    return pltpu.make_async_remote_copy(
        src_ref=src, dst_ref=dst, send_sem=send_sem, recv_sem=recv_sem, device_id=to, device_id_type=MESH
    )


def spread_channels(values):
    width = NZL * CB
    rows = lax.broadcasted_iota(jnp.int32, (NY * width, NY * 128), 0)
    cols = lax.broadcasted_iota(jnp.int32, (NY * width, NY * 128), 1)
    block, lane = cols // 128, cols % 128
    chosen = jnp.where((lane < width) & (rows == block * width + lane), 1.0, 0.0).astype(BF16)
    return jnp.dot(values, chosen, preferred_element_type=F32).astype(BF16)


def reduce_scratch():
    lanes = NY * 128
    return dict(
        own=pltpu.VMEM((2, NZH, NX, HB, lanes), F32),
        b1=pltpu.VMEM((2, NZH, NX, HB, lanes), BF16),
        r1=pltpu.VMEM((2, NZH, NX, HB, lanes), BF16),
        b2d=pltpu.VMEM((NX, NZH, HB, lanes), BF16),
        r2d=pltpu.VMEM((NX - 1, NZH, HB, lanes), BF16),
        b2u=pltpu.VMEM((NY, NZH, NX, HB, 128), BF16),
        r2u=pltpu.VMEM((NY - 1, NZH, NX, HB, 128), BF16),
        a3u=pltpu.VMEM((NX, NZH, HB, 128), F32),
        b3d=pltpu.VMEM((NY, NZH, HB, 128), BF16),
        r3d=pltpu.VMEM((NY - 1, NZH, HB, 128), BF16),
        b3u=pltpu.VMEM((NX, NZH, HB, 128), BF16),
        r3u=pltpu.VMEM((NX - 1, NZH, HB, 128), BF16),
        b4=pltpu.VMEM((NZL, NZH, 16, 128), BF16),
        r4=pltpu.VMEM((NZL - 1, NZH, 16, 128), BF16),
        a5=pltpu.VMEM((NZH, 16, 128), F32),
        b5=pltpu.VMEM((NZH, 16, 128), BF16),
        b6=pltpu.VMEM((16, 128), BF16),
        r5=pltpu.VMEM((3, 16, 128), BF16),
        total=pltpu.VMEM((2, NZH, NX * NC * HB, lanes), F32),
        s1=pltpu.SemaphoreType.DMA((2, 2, NZH)),
        s2d=pltpu.SemaphoreType.DMA((2, NX - 1, NZH)),
        s2u=pltpu.SemaphoreType.DMA((2, NY - 1, NZH)),
        s3d=pltpu.SemaphoreType.DMA((2, NY - 1)),
        s3u=pltpu.SemaphoreType.DMA((2, NX - 1)),
        s4=pltpu.SemaphoreType.DMA((2, NZL - 1)),
        s5=pltpu.SemaphoreType.DMA((2, 3)),
    )


DOWN, UP = 0, 1


class Reduction:
    def __init__(self, peers, refs):
        self.peers = peers
        self.__dict__.update(refs)

    def first_copy(self, g, z):
        return send(self.b1.at[g, z], self.r1.at[g, z], self.s1.at[0, g, z], self.s1.at[1, g, z], self.peers.core())

    def term(self, g, z, left, right, last):
        core = self.peers.at[2]
        value = lax.dot_general(left, right, (((0,), (0,)), ((), ())), preferred_element_type=F32)

        if not last:
            self.total[g, z] = value
        else:
            whole = (value + self.total[g, z]).reshape(NX, NC, HB, NY * 128)
            self.own[g, z] = jnp.where(core == 0, whole[:, 0], whole[:, 1])
            self.b1[g, z] = jnp.where(core == 0, whole[:, 1], whole[:, 0]).astype(BF16)
            self.first_copy(g, z).start()

    def second_copies(self, g, z):
        p = self.peers
        if g == DOWN:
            for k in range(1, NX):
                to, there = p.x(k)
                yield send(self.b2d.at[to, z], self.r2d.at[k - 1, z], self.s2d.at[0, k - 1, z], self.s2d.at[1, k - 1, z], there)
        else:
            for k in range(1, NY):
                to, there = p.y(k)
                yield send(self.b2u.at[to, z], self.r2u.at[k - 1, z], self.s2u.at[0, k - 1, z], self.s2u.at[1, k - 1, z], there)

    def second(self, g, z):
        self.first_copy(g, z).wait_recv()
        value = self.own[g, z] + self.r1[g, z].astype(F32)
        self.own[g, z] = value
        if g == DOWN:
            for x in range(NX):
                self.b2d[x, z] = value[x].astype(BF16)
        else:
            for y in range(NY):
                self.b2u[y, z] = value[:, :, y * 128 : (y + 1) * 128].astype(BF16)
        for copy in self.second_copies(g, z):
            copy.start()

    def third_copies(self, g):
        p = self.peers
        if g == DOWN:
            for k in range(1, NY):
                to, there = p.y(k)
                yield send(self.b3d.at[to], self.r3d.at[k - 1], self.s3d.at[0, k - 1], self.s3d.at[1, k - 1], there)
        else:
            for k in range(1, NX):
                to, there = p.x(k)
                yield send(self.b3u.at[to], self.r3u.at[k - 1], self.s3u.at[0, k - 1], self.s3u.at[1, k - 1], there)

    def third_sum(self, g, z):
        zh, x, c, y, zl = self.peers.at
        for copy in self.second_copies(g, z):
            copy.wait_recv()
        if g == DOWN:
            value = self.own[g, z, x]
            for k in range(NX - 1):
                value = value + self.r2d[k, z].astype(F32)
            self.own[g, z, x] = value
            for j in range(NY):
                self.b3d[j, z] = value[:, j * 128 : (j + 1) * 128].astype(BF16)
        else:
            value = self.own[g, z, :, :, pl.ds(pl.multiple_of(y * 128, 128), 128)]
            for k in range(NY - 1):
                value = value + self.r2u[k, z].astype(F32)
            for j in range(NX):
                self.a3u[j, z] = value[j]
                self.b3u[j, z] = value[j].astype(BF16)

    def third(self, g):
        @pl.loop(0, NZH)
        def _(z):
            self.third_sum(g, z)

        for copy in self.third_copies(g):
            copy.start()

    def fourth_copies(self):
        for k in range(1, NZL):
            to, there = self.peers.zl(k)
            yield send(self.b4.at[to], self.r4.at[k - 1], self.s4.at[0, k - 1], self.s4.at[1, k - 1], there)

    def fourth(self):
        zh, x, c, y, zl = self.peers.at
        for g in (DOWN, UP):
            for copy in self.third_copies(g):
                copy.wait_recv()
        shape = (NZL * 16, 128)
        rows, cols = lax.broadcasted_iota(jnp.int32, shape, 0), lax.broadcasted_iota(jnp.int32, shape, 1)
        chosen = jnp.where((rows % 16 < CB) & (cols == (rows // 16) * CB + rows % 16), 1.0, 0.0).astype(BF16)

        @pl.loop(0, NZH)
        def _(z):
            up = self.a3u[x, z]
            for k in range(NX - 1):
                up = up + self.r3u[k, z].astype(F32)
            down = self.own[DOWN, z, x, :, pl.ds(pl.multiple_of(y * 128, 128), 128)]
            for k in range(NY - 1):
                down = down + self.r3d[k, z].astype(F32)
            both = jnp.concatenate([up, down, jnp.zeros((128 - 2 * HB, 128), F32)], axis=0).astype(BF16)
            placed = lax.dot_general(chosen, both, (((1,), (1,)), ((), ())), preferred_element_type=F32)
            placed = placed.reshape(NZL, 16, 128).astype(BF16)
            for j in range(NZL):
                self.b4[j, z] = placed[j]

        for copy in self.fourth_copies():
            copy.start()

    def fifth_copies(self):
        to, there = self.peers.zh(0)
        for k, block in enumerate((to, NZH - 1 - to)):
            yield send(self.b5.at[block], self.r5.at[k], self.s5.at[0, k], self.s5.at[1, k], there)

    def sixth_copy(self):
        to, there = self.peers.zh(1)
        return send(self.b6, self.r5.at[2], self.s5.at[0, 2], self.s5.at[1, 2], there)

    def fifth(self):
        zl = self.peers.at[4]
        value = self.b4[zl].astype(F32)
        for k, copy in enumerate(self.fourth_copies()):
            copy.wait_recv()
            value = value + self.r4[k].astype(F32)
        self.a5[...] = value
        self.b5[...] = value.astype(BF16)
        for copy in self.fifth_copies():
            copy.start()

    def sixth(self):
        zh = self.peers.at[0]
        for copy in self.fifth_copies():
            copy.wait_recv()
        self.b6[...] = (self.a5[NZH - 1 - zh] + self.r5[1].astype(F32)).astype(BF16)
        self.sixth_copy().start()

    def finish(self, factor, up_ref, down_ref):
        zh = self.peers.at[0]
        value = self.a5[zh] + self.r5[0].astype(F32)
        self.sixth_copy().wait_recv()
        value = (value + self.r5[2].astype(F32)) * factor
        up_ref[...] = value[:CB, :HB]
        down_ref[...] = pltpu.roll(value, 128 - HB, 1)[:CB, :HB]

    def drain(self):
        @pl.loop(0, NZH)
        def _(z):
            for g in (DOWN, UP):
                self.first_copy(g, z).wait_send()
                for copy in self.second_copies(g, z):
                    copy.wait_send()

        for g in (DOWN, UP):
            for copy in self.third_copies(g):
                copy.wait_send()
        for copy in self.fourth_copies():
            copy.wait_send()
        for copy in self.fifth_copies():
            copy.wait_send()
        self.sixth_copy().wait_send()


KS, REACH = 7, 3
HROWS, COLS = 8, 64
PARTS = (HROWS - REACH, REACH)
MOST = PARTS[0] * COLS


def row_sum(rows, kernel_ref, lanes, flip):
    col = lax.broadcasted_iota(jnp.int32, (COLS, 128), 0)
    total = None
    for j in range(KS):
        part = None
        for value, i in rows:
            a, b = (KS - 1 - i, KS - 1 - j) if flip else (i, j)
            tap = value * kernel_ref[a, b : b + 1, lanes]
            part = tap if part is None else part + tap
        shift = j - REACH
        if shift != 0:
            inside = (col + shift >= 0) & (col + shift < COLS)
            part = jnp.where(inside, pltpu.roll(part, (-shift) % COLS, 0), 0.0)
        total = part if total is None else total + part
    return total


def own_rows(source, sums, kernel_ref, flip):
    @pl.loop(0, source.shape[2] // 128)
    def _(block):
        lanes = pl.ds(pl.multiple_of(block * 128, 128), 128)

        @pl.loop(0, HROWS)
        def _(h):
            rows = [(source[h + i, :, lanes], i) for i in range(KS)]
            sums[h, :, lanes] = row_sum(rows, kernel_ref, lanes, flip)


def halo_rows(halo, side, sums, kernel_ref, flip):
    for static_side in (0, 1):

        @pl.when(side == static_side)
        def _(static_side=static_side):
            @pl.loop(0, sums.shape[2] // 128)
            def _(block):
                lanes = pl.ds(pl.multiple_of(block * 128, 128), 128)
                rows = [halo[static_side, r * COLS : (r + 1) * COLS, lanes].astype(F32) for r in range(REACH)]
                for h in range(REACH):
                    if static_side == 0:
                        used, at = [(rows[r], r - h) for r in range(h, REACH)], h
                    else:
                        used, at = [(rows[r], KS - 1 + r - h) for r in range(h + 1)], HROWS - REACH + h
                    sums[at, :, lanes] = sums[at, :, lanes] + row_sum(used, kernel_ref, lanes, flip)


def gelu_parts(values):
    denominator = 1.0 + 0.2316419 * jnp.abs(values)
    guess = pl.reciprocal(denominator, approx=True)
    t = guess * (2.0 - denominator * guess)
    density = jnp.exp2(values * values * (-0.5 * math.log2(math.e))) * (1.0 / math.sqrt(2.0 * math.pi))
    series = t * (0.319381530 + t * (-0.356563782 + t * (1.781477937 + t * (-1.821255978 + t * 1.330274429))))
    tail = density * series
    cdf = jnp.where(values >= 0.0, 1.0 - tail, tail)
    return values * cdf, cdf + values * density


def block_kernel(factor, names, images, kernel, conv_bias, gain, shift, up_whole, up_bias, down_whole, scale, cotangent,
                 out, up_out, down_out, *scratch):
    s = dict(zip(names, scratch))
    peers = Peers()
    others = peers.all()
    greet(others)
    sums = Reduction(peers, s)
    zh, x, c, y, zl = peers.at
    strip = (zh * NX + x) * NC + c
    up_weight, down_weight = s["up_weight"], s["down_weight"]
    down_copy = pltpu.make_async_copy(down_whole, down_weight, s["weight_sems"].at[0])
    up_copy = pltpu.make_async_copy(up_whole, up_weight, s["weight_sems"].at[1])
    down_copy.start()
    up_copy.start()
    channels, hidden = up_weight.shape
    width = NX * NC * HB
    source, gradient, conv = s["source"], s["gradient"], s["conv"]
    scaled, spread_scaled, grad_act = s["scaled"], s["spread_scaled"], s["grad_act"]
    standard, inverse, normed, spread_normed = s["standard"], s["inverse"], s["normed"], s["spread_normed"]
    before, activated, slope, grad_normed, grad_conv = s["before"], s["activated"], s["slope"], s["grad_normed"], s["grad_conv"]

    def row(vector):
        return vector[...].reshape(1, channels)

    def chunk(n):
        return pl.ds(pl.multiple_of(n * width, 128), width)

    def has_neighbour(side):
        return jnp.where(side == 0, strip > 0, strip < NROWS - 1)

    def halo_copy(strip_ref, halo, sems, side):
        first = pl.multiple_of(side * ((HROWS - REACH) * COLS), COLS)
        return send(strip_ref.at[pl.ds(first, REACH * COLS)], halo.at[1 - side], sems.at[0, side], sems.at[1, 1 - side],
                    peers.strip(2 * side - 1))

    def arrived(strip_ref, halo, sems, side):
        halo_copy(strip_ref, halo, sems, 1 - side).wait_recv()

    for rows in (source, gradient):
        rows[:REACH] = jnp.zeros((REACH, COLS, channels), F32)
        rows[REACH + HROWS :] = jnp.zeros((REACH, COLS, channels), F32)

    @pl.loop(0, HROWS)
    def _(h):
        at = pl.ds(pl.multiple_of(h * COLS, COLS), COLS)
        source[REACH + h] = images[at, :].astype(F32)
        scaled[at, :] = (cotangent[at, :].astype(F32) * row(scale)).astype(BF16)

    own_rows(source, conv, kernel, False)
    spread_scaled[...] = spread_channels(scaled[...])

    await_greetings(others)
    for side in (0, 1):

        @pl.when(has_neighbour(side))
        def _(side=side):
            halo_copy(images, s["image_halo"], s["image_sems"], side).start()

    down_copy.wait()

    @pl.loop(0, NZH)
    def _(n):
        grad_act[:, chunk(n)] = jnp.dot(scaled[...], down_weight[:, chunk(n)], preferred_element_type=F32)

    up_copy.wait()
    early = jnp.where((x == 0) & (c == 0), 1, 0)

    def part(rows, first, side, last):
        size = rows * COLS

        @pl.when(has_neighbour(side))
        def _():
            arrived(images, s["image_halo"], s["image_sems"], side)
            halo_rows(s["image_halo"], side, conv, kernel, False)

        pixels = pl.ds(pl.multiple_of(first * COLS, COLS), size)

        @pl.loop(0, rows)
        def _(k):
            h = first + k
            at = pl.ds(pl.multiple_of(h * COLS, COLS), COLS)
            value = conv[h] + row(conv_bias)
            centered = value - jnp.sum(value, axis=1, keepdims=True) * (1.0 / channels)
            inv = lax.rsqrt(jnp.sum(centered * centered, axis=1, keepdims=True) * (1.0 / channels) + EPSILON)
            std = centered * inv
            standard[at, :] = std
            inverse[at, :] = inv
            normed[at, :] = (std * row(gain) + row(shift)).astype(BF16)

        spread_normed[:size] = spread_channels(normed[pixels, :])

        @pl.loop(0, NZH)
        def _(n):
            weights = up_weight[:, chunk(n)]
            before[:size] = jnp.dot(normed[pixels, :], weights, preferred_element_type=F32)

            @pl.loop(0, size // TILE)
            def _(k):
                at = pl.ds(pl.multiple_of(k * TILE, TILE), TILE)
                act, slopes = gelu_parts(before[at, :] + up_bias[chunk(n)].reshape(1, width))
                activated[at, :] = act.astype(BF16)
                grads = grad_act[pl.ds(pl.multiple_of(first * COLS + k * TILE, TILE), TILE), chunk(n)]
                slope[at, :] = (grads * slopes).astype(BF16)

            sums.term(DOWN, n, activated[:size], spread_scaled[pixels, :], last)
            sums.term(UP, n, slope[:size], spread_normed[:size], last)
            back = lax.dot_general(slope[:size], weights, (((1,), (1,)), ((), ())), preferred_element_type=F32)

            @pl.when(n == 0)
            def _():
                grad_normed[:size] = back

            @pl.when(n > 0)
            def _():
                grad_normed[:size] = grad_normed[:size] + back

            if last:

                @pl.when(n > 0)
                def _():
                    sums.second(DOWN, n - 1)
                    sums.second(UP, n - 1)

        @pl.loop(0, rows)
        def _(k):
            h = first + k
            at = pl.ds(pl.multiple_of(h * COLS, COLS), COLS)
            gscaled = grad_normed[pl.ds(pl.multiple_of(k * COLS, COLS), COLS), :] * row(gain)
            std = standard[at, :]
            mean = jnp.sum(gscaled, axis=1, keepdims=True) * (1.0 / channels)
            along = jnp.sum(gscaled * std, axis=1, keepdims=True) * (1.0 / channels)
            value = (inverse[at, :] * (gscaled - mean - std * along)).astype(BF16)
            grad_conv[at, :] = value
            gradient[REACH + h] = value.astype(F32)

        @pl.when(has_neighbour(side))
        def _():
            halo_copy(grad_conv, s["grad_halo"], s["grad_sems"], side).start()

    part(PARTS[0], early * REACH, early, False)
    part(PARTS[1], (1 - early) * PARTS[0], 1 - early, True)
    for g in (DOWN, UP):
        sums.second(g, NZH - 1)
    own_rows(gradient, conv, kernel, True)
    for g in (DOWN, UP):
        sums.third(g)
    sums.fourth()
    for step in (0, 1):
        side = jnp.where(step == 0, early, 1 - early)

        @pl.when(has_neighbour(side))
        def _(side=side):
            arrived(grad_conv, s["grad_halo"], s["grad_sems"], side)
            halo_rows(s["grad_halo"], side, conv, kernel, True)

    @pl.loop(0, HROWS)
    def _(h):
        at = pl.ds(pl.multiple_of(h * COLS, COLS), COLS)
        out[at, :] = (cotangent[at, :].astype(F32) + conv[h]).astype(BF16)

    sums.fifth()
    sums.sixth()
    sums.finish(factor, up_out, down_out)
    sums.drain()
    for strip_ref, halo, sems in ((images, s["image_halo"], s["image_sems"]), (grad_conv, s["grad_halo"], s["grad_sems"])):
        for side in (0, 1):

            @pl.when(has_neighbour(side))
            def _(strip_ref=strip_ref, halo=halo, sems=sems, side=side):
                halo_copy(strip_ref, halo, sems, side).wait_send()


TILE = 64


def hand_over(images, up, down, images_out, up_out, down_out):
    images_out[...] = images[...]
    up_out[...] = up[...]
    down_out[...] = down[...]


def on_device(
    images,
    kernel,
    conv_bias,
    norm_gain,
    norm_shift,
    up_weight,
    up_bias,
    down_weight,
    layer_scale,
    cotangent,
):
    shape = images.shape
    channels, hidden = up_weight.shape
    pixels = shape[0] * shape[1] * shape[2]
    groups, parts = lax.axis_size("dp"), lax.axis_size("rows")
    factor = 1.0 / math.sqrt(pixels * groups * parts)
    scratch = reduce_scratch() | dict(
        source=pltpu.VMEM((HROWS + 2 * REACH, COLS, channels), F32),
        gradient=pltpu.VMEM((HROWS + 2 * REACH, COLS, channels), F32),
        conv=pltpu.VMEM((HROWS, COLS, channels), F32),
        up_weight=pltpu.VMEM(up_weight.shape, BF16),
        down_weight=pltpu.VMEM(down_weight.shape, BF16),
        weight_sems=pltpu.SemaphoreType.DMA((2,)),
        scaled=pltpu.VMEM((pixels, channels), BF16),
        spread_scaled=pltpu.VMEM((pixels, NY * 128), BF16),
        grad_act=pltpu.VMEM((pixels, hidden), F32),
        standard=pltpu.VMEM((pixels, channels), F32),
        inverse=pltpu.VMEM((pixels, 1), F32),
        normed=pltpu.VMEM((pixels, channels), BF16),
        spread_normed=pltpu.VMEM((MOST, NY * 128), BF16),
        before=pltpu.VMEM((MOST, NX * NC * HB), F32),
        activated=pltpu.VMEM((MOST, NX * NC * HB), BF16),
        slope=pltpu.VMEM((MOST, NX * NC * HB), BF16),
        grad_normed=pltpu.VMEM((MOST, channels), F32),
        grad_conv=pltpu.VMEM((pixels, channels), BF16),
        image_halo=pltpu.VMEM((2, REACH * COLS, channels), BF16),
        grad_halo=pltpu.VMEM((2, REACH * COLS, channels), BF16),
        image_sems=pltpu.SemaphoreType.DMA((2, 2)),
        grad_sems=pltpu.SemaphoreType.DMA((2, 2)),
    )
    block = jax.ShapeDtypeStruct((CB, HB), F32)
    vmem, anywhere = pl.BlockSpec(memory_space=pltpu.VMEM), pl.BlockSpec(memory_space=pl.ANY)
    grad_images, grad_up, grad_down = pl.pallas_call(
        functools.partial(block_kernel, factor, tuple(scratch)),
        out_shape=(jax.ShapeDtypeStruct((pixels, channels), BF16), block, block),
        in_specs=[vmem] * 5 + [anywhere, vmem, anywhere, vmem, vmem],
        out_specs=(vmem, vmem, vmem),
        scratch_shapes=list(scratch.values()),
        compiler_params=pltpu.CompilerParams(
            collective_id=0, has_side_effects=True, vmem_limit_bytes=56 * 1024 * 1024
        ),
    )(
        images.reshape(pixels, channels),
        kernel,
        conv_bias,
        norm_gain,
        norm_shift,
        up_weight,
        up_bias,
        down_weight,
        layer_scale,
        cotangent.reshape(pixels, channels),
    )
    grad_images, grad_up, grad_down = pl.pallas_call(
        hand_over,
        out_shape=(jax.ShapeDtypeStruct((pixels, channels), BF16), block, block),
        in_specs=[vmem] * 3,
        out_specs=(vmem, vmem, vmem),
    )(grad_images, grad_up, grad_down)
    return (grad_images.reshape(shape), grad_up, grad_down)


def solution(mesh):
    in_specs = (
        P("dp", "rows", None, None),
        P(),
        P(),
        P(),
        P(),
        P(),
        P(),
        P(),
        P(),
        P("dp", "rows", None, None),
    )
    out_specs = (P("dp", "rows", None, None), P("dp", "rows"), P("dp", "rows"))
    return jax.shard_map(
        on_device, mesh=mesh, in_specs=in_specs, out_specs=out_specs, check_vma=False
    )
```

```python
import functools
import math

import jax
import jax.numpy as jnp
from jax import lax
from jax.experimental import pallas as pl
from jax.experimental.pallas import tpu as pltpu
from jax.sharding import PartitionSpec as P

EPSILON = 1e-06
MESH = pl.DeviceIdType.MESH
F32 = jnp.float32
BF16 = jnp.bfloat16

NZH, NX, NC, NY, NZL = 4, 4, 2, 4, 8
NROWS = NZH * NX * NC
HB, CB = 48, 12


def coordinates():
    dp, rows = lax.axis_index("dp"), lax.axis_index("rows")
    core, chip = lax.rem(rows, NC), lax.div(rows, NC)
    return (
        lax.div(chip, NX),
        lax.rem(chip, NX),
        core,
        lax.div(dp, NZL),
        lax.rem(dp, NZL),
    )


def device(zh, x, c, y, zl):
    return (y * NZL + zl, (zh * NX + x) * NC + c)


def around(place, step, count):
    return lax.rem(place + step, count)


class Peers:
    def __init__(self):
        self.at = coordinates()

    def core(self):
        zh, x, c, y, zl = self.at
        return device(zh, x, 1 - c, y, zl)

    def x(self, k):
        zh, x, c, y, zl = self.at
        to = around(x, k, NX)
        return to, device(zh, to, c, y, zl)

    def y(self, k):
        zh, x, c, y, zl = self.at
        to = around(y, k, NY)
        return to, device(zh, x, c, to, zl)

    def zl(self, k):
        zh, x, c, y, zl = self.at
        to = around(zl, k, NZL)
        return to, device(zh, x, c, y, to)

    def zh(self, k):
        zh, x, c, y, zl = self.at
        to = zh + 1 - 2 * lax.rem(zh, 2) if k == 0 else NZH - 1 - zh
        return to, device(to, x, c, y, zl)

    def strip(self, step):
        zh, x, c, y, zl = self.at
        row = around((zh * NX + x) * NC + c, step + NROWS, NROWS)
        return (y * NZL + zl, row)

    def all(self):
        found = [self.core(), self.strip(-1), self.strip(1), self.zh(0)[1], self.zh(1)[1]]
        for way, count in ((self.x, NX), (self.y, NY), (self.zl, NZL)):
            found += [way(k)[1] for k in range(1, count)]
        return found


def greet(others):
    barrier = pltpu.get_barrier_semaphore()
    for other in others:
        pl.semaphore_signal(barrier, inc=1, device_id=other, device_id_type=MESH)


def await_greetings(others):
    pl.semaphore_wait(pltpu.get_barrier_semaphore(), len(others))


def send(src, dst, send_sem, recv_sem, to):
    return pltpu.make_async_remote_copy(
        src_ref=src, dst_ref=dst, send_sem=send_sem, recv_sem=recv_sem, device_id=to, device_id_type=MESH
    )


def spread_channels(values):
    width = NZL * CB
    rows = lax.broadcasted_iota(jnp.int32, (NY * width, NY * 128), 0)
    cols = lax.broadcasted_iota(jnp.int32, (NY * width, NY * 128), 1)
    block, lane = cols // 128, cols % 128
    chosen = jnp.where((lane < width) & (rows == block * width + lane), 1.0, 0.0).astype(BF16)
    return jnp.dot(values, chosen, preferred_element_type=F32).astype(BF16)


def reduce_scratch():
    lanes = NY * 128
    return dict(
        own=pltpu.VMEM((2, NZH, NX, HB, lanes), F32),
        b1=pltpu.VMEM((2, NZH, NX, HB, lanes), BF16),
        r1=pltpu.VMEM((2, NZH, NX, HB, lanes), BF16),
        b2d=pltpu.VMEM((NX, NZH, HB, lanes), BF16),
        r2d=pltpu.VMEM((NX - 1, NZH, HB, lanes), BF16),
        b2u=pltpu.VMEM((NY, NZH, NX, HB, 128), BF16),
        r2u=pltpu.VMEM((NY - 1, NZH, NX, HB, 128), BF16),
        a3u=pltpu.VMEM((NX, NZH, HB, 128), F32),
        b3d=pltpu.VMEM((NY, NZH, HB, 128), BF16),
        r3d=pltpu.VMEM((NY - 1, NZH, HB, 128), BF16),
        b3u=pltpu.VMEM((NX, NZH, HB, 128), BF16),
        r3u=pltpu.VMEM((NX - 1, NZH, HB, 128), BF16),
        b4=pltpu.VMEM((NZL, NZH, 16, 128), BF16),
        r4=pltpu.VMEM((NZL - 1, NZH, 16, 128), BF16),
        a5=pltpu.VMEM((NZH, 16, 128), F32),
        b5=pltpu.VMEM((NZH, 16, 128), BF16),
        b6=pltpu.VMEM((16, 128), BF16),
        r5=pltpu.VMEM((3, 16, 128), BF16),
        total=pltpu.VMEM((2, NZH, NX * NC * HB, lanes), F32),
        s1=pltpu.SemaphoreType.DMA((2, 2, NZH)),
        s2d=pltpu.SemaphoreType.DMA((2, NX - 1, NZH)),
        s2u=pltpu.SemaphoreType.DMA((2, NY - 1, NZH)),
        s3d=pltpu.SemaphoreType.DMA((2, NY - 1)),
        s3u=pltpu.SemaphoreType.DMA((2, NX - 1)),
        s4=pltpu.SemaphoreType.DMA((2, NZL - 1)),
        s5=pltpu.SemaphoreType.DMA((2, 3)),
    )


DOWN, UP = 0, 1


class Reduction:
    def __init__(self, peers, refs):
        self.peers = peers
        self.__dict__.update(refs)

    def first_copy(self, g, z):
        return send(self.b1.at[g, z], self.r1.at[g, z], self.s1.at[0, g, z], self.s1.at[1, g, z], self.peers.core())

    def term(self, g, z, left, right, last):
        core = self.peers.at[2]
        value = lax.dot_general(left, right, (((0,), (0,)), ((), ())), preferred_element_type=F32)

        if not last:
            self.total[g, z] = value
        else:
            whole = (value + self.total[g, z]).reshape(NX, NC, HB, NY * 128)
            self.own[g, z] = jnp.where(core == 0, whole[:, 0], whole[:, 1])
            self.b1[g, z] = jnp.where(core == 0, whole[:, 1], whole[:, 0]).astype(BF16)
            self.first_copy(g, z).start()

    def second_copies(self, g, z):
        p = self.peers
        if g == DOWN:
            for k in range(1, NX):
                to, there = p.x(k)
                yield send(self.b2d.at[to, z], self.r2d.at[k - 1, z], self.s2d.at[0, k - 1, z], self.s2d.at[1, k - 1, z], there)
        else:
            for k in range(1, NY):
                to, there = p.y(k)
                yield send(self.b2u.at[to, z], self.r2u.at[k - 1, z], self.s2u.at[0, k - 1, z], self.s2u.at[1, k - 1, z], there)

    def second(self, g, z):
        self.first_copy(g, z).wait_recv()
        value = self.own[g, z] + self.r1[g, z].astype(F32)
        self.own[g, z] = value
        if g == DOWN:
            for x in range(NX):
                self.b2d[x, z] = value[x].astype(BF16)
        else:
            for y in range(NY):
                self.b2u[y, z] = value[:, :, y * 128 : (y + 1) * 128].astype(BF16)
        for copy in self.second_copies(g, z):
            copy.start()

    def third_copies(self, g):
        p = self.peers
        if g == DOWN:
            for k in range(1, NY):
                to, there = p.y(k)
                yield send(self.b3d.at[to], self.r3d.at[k - 1], self.s3d.at[0, k - 1], self.s3d.at[1, k - 1], there)
        else:
            for k in range(1, NX):
                to, there = p.x(k)
                yield send(self.b3u.at[to], self.r3u.at[k - 1], self.s3u.at[0, k - 1], self.s3u.at[1, k - 1], there)

    def third_sum(self, g, z):
        zh, x, c, y, zl = self.peers.at
        for copy in self.second_copies(g, z):
            copy.wait_recv()
        if g == DOWN:
            value = self.own[g, z, x]
            for k in range(NX - 1):
                value = value + self.r2d[k, z].astype(F32)
            self.own[g, z, x] = value
            for j in range(NY):
                self.b3d[j, z] = value[:, j * 128 : (j + 1) * 128].astype(BF16)
        else:
            value = self.own[g, z, :, :, pl.ds(pl.multiple_of(y * 128, 128), 128)]
            for k in range(NY - 1):
                value = value + self.r2u[k, z].astype(F32)
            for j in range(NX):
                self.a3u[j, z] = value[j]
                self.b3u[j, z] = value[j].astype(BF16)

    def third(self, g):
        @pl.loop(0, NZH)
        def _(z):
            self.third_sum(g, z)

        for copy in self.third_copies(g):
            copy.start()

    def fourth_copies(self):
        for k in range(1, NZL):
            to, there = self.peers.zl(k)
            yield send(self.b4.at[to], self.r4.at[k - 1], self.s4.at[0, k - 1], self.s4.at[1, k - 1], there)

    def fourth(self):
        zh, x, c, y, zl = self.peers.at
        for g in (DOWN, UP):
            for copy in self.third_copies(g):
                copy.wait_recv()
        shape = (NZL * 16, 128)
        rows, cols = lax.broadcasted_iota(jnp.int32, shape, 0), lax.broadcasted_iota(jnp.int32, shape, 1)
        chosen = jnp.where((rows % 16 < CB) & (cols == (rows // 16) * CB + rows % 16), 1.0, 0.0).astype(BF16)

        @pl.loop(0, NZH)
        def _(z):
            up = self.a3u[x, z]
            for k in range(NX - 1):
                up = up + self.r3u[k, z].astype(F32)
            down = self.own[DOWN, z, x, :, pl.ds(pl.multiple_of(y * 128, 128), 128)]
            for k in range(NY - 1):
                down = down + self.r3d[k, z].astype(F32)
            both = jnp.concatenate([up, down, jnp.zeros((128 - 2 * HB, 128), F32)], axis=0).astype(BF16)
            placed = lax.dot_general(chosen, both, (((1,), (1,)), ((), ())), preferred_element_type=F32)
            placed = placed.reshape(NZL, 16, 128).astype(BF16)
            for j in range(NZL):
                self.b4[j, z] = placed[j]

        for copy in self.fourth_copies():
            copy.start()

    def fifth_copies(self):
        to, there = self.peers.zh(0)
        for k, block in enumerate((to, NZH - 1 - to)):
            yield send(self.b5.at[block], self.r5.at[k], self.s5.at[0, k], self.s5.at[1, k], there)

    def sixth_copy(self):
        to, there = self.peers.zh(1)
        return send(self.b6, self.r5.at[2], self.s5.at[0, 2], self.s5.at[1, 2], there)

    def fifth(self):
        zl = self.peers.at[4]
        value = self.b4[zl].astype(F32)
        for k, copy in enumerate(self.fourth_copies()):
            copy.wait_recv()
            value = value + self.r4[k].astype(F32)
        self.a5[...] = value
        self.b5[...] = value.astype(BF16)
        for copy in self.fifth_copies():
            copy.start()

    def sixth(self):
        zh = self.peers.at[0]
        for copy in self.fifth_copies():
            copy.wait_recv()
        self.b6[...] = (self.a5[NZH - 1 - zh] + self.r5[1].astype(F32)).astype(BF16)
        self.sixth_copy().start()

    def finish(self, factor, up_ref, down_ref):
        zh = self.peers.at[0]
        value = self.a5[zh] + self.r5[0].astype(F32)
        self.sixth_copy().wait_recv()
        value = (value + self.r5[2].astype(F32)) * factor
        up_ref[...] = value[:CB, :HB]
        down_ref[...] = pltpu.roll(value, 128 - HB, 1)[:CB, :HB]

    def drain(self):
        @pl.loop(0, NZH)
        def _(z):
            for g in (DOWN, UP):
                self.first_copy(g, z).wait_send()
                for copy in self.second_copies(g, z):
                    copy.wait_send()

        for g in (DOWN, UP):
            for copy in self.third_copies(g):
                copy.wait_send()
        for copy in self.fourth_copies():
            copy.wait_send()
        for copy in self.fifth_copies():
            copy.wait_send()
        self.sixth_copy().wait_send()


KS, REACH = 7, 3
HROWS, COLS = 8, 64
PARTS = (HROWS - REACH, REACH)
MOST = PARTS[0] * COLS


def row_sum(rows, kernel_ref, lanes, flip):
    col = lax.broadcasted_iota(jnp.int32, (COLS, 128), 0)
    total = None
    for j in range(KS):
        part = None
        for value, i in rows:
            a, b = (KS - 1 - i, KS - 1 - j) if flip else (i, j)
            tap = value * kernel_ref[a, b : b + 1, lanes]
            part = tap if part is None else part + tap
        shift = j - REACH
        if shift != 0:
            inside = (col + shift >= 0) & (col + shift < COLS)
            part = jnp.where(inside, pltpu.roll(part, (-shift) % COLS, 0), 0.0)
        total = part if total is None else total + part
    return total


def own_rows(source, sums, kernel_ref, flip):
    @pl.loop(0, source.shape[2] // 128)
    def _(block):
        lanes = pl.ds(pl.multiple_of(block * 128, 128), 128)

        @pl.loop(0, HROWS)
        def _(h):
            rows = [(source[h + i, :, lanes], i) for i in range(KS)]
            sums[h, :, lanes] = row_sum(rows, kernel_ref, lanes, flip)


def halo_rows(halo, side, sums, kernel_ref, flip):
    for static_side in (0, 1):

        @pl.when(side == static_side)
        def _(static_side=static_side):
            @pl.loop(0, sums.shape[2] // 128)
            def _(block):
                lanes = pl.ds(pl.multiple_of(block * 128, 128), 128)
                rows = [halo[static_side, r * COLS : (r + 1) * COLS, lanes].astype(F32) for r in range(REACH)]
                for h in range(REACH):
                    if static_side == 0:
                        used, at = [(rows[r], r - h) for r in range(h, REACH)], h
                    else:
                        used, at = [(rows[r], KS - 1 + r - h) for r in range(h + 1)], HROWS - REACH + h
                    sums[at, :, lanes] = sums[at, :, lanes] + row_sum(used, kernel_ref, lanes, flip)


def gelu_parts(values):
    denominator = 1.0 + 0.2316419 * jnp.abs(values)
    guess = pl.reciprocal(denominator, approx=True)
    t = guess * (2.0 - denominator * guess)
    density = jnp.exp2(values * values * (-0.5 * math.log2(math.e))) * (1.0 / math.sqrt(2.0 * math.pi))
    series = t * (0.319381530 + t * (-0.356563782 + t * (1.781477937 + t * (-1.821255978 + t * 1.330274429))))
    tail = density * series
    cdf = jnp.where(values >= 0.0, 1.0 - tail, tail)
    return values * cdf, cdf + values * density


def block_kernel(factor, names, images_whole, kernel, conv_bias, gain, shift, up_whole, up_bias, down_whole, scale,
                 cotangent_whole, out_whole, up_out, down_out, *scratch):
    s = dict(zip(names, scratch))
    peers = Peers()
    others = peers.all()
    greet(others)
    sums = Reduction(peers, s)
    zh, x, c, y, zl = peers.at
    strip = (zh * NX + x) * NC + c
    images, cotangent, up_weight, down_weight, out = (
        s[name] for name in ("images", "cotangent", "up_weight", "down_weight", "out")
    )
    loads = ((images_whole, images), (cotangent_whole, cotangent), (down_whole, down_weight), (up_whole, up_weight))
    loads = [pltpu.make_async_copy(*pair, s["load_sems"].at[k]) for k, pair in enumerate(loads)]
    store = pltpu.make_async_copy(out, out_whole, s["load_sems"].at[len(loads)])
    for load in loads:
        load.start()
    channels, hidden = up_weight.shape
    width = NX * NC * HB
    source, gradient, conv = s["source"], s["gradient"], s["conv"]
    scaled, spread_scaled, grad_act = s["scaled"], s["spread_scaled"], s["grad_act"]
    standard, inverse, normed, spread_normed = s["standard"], s["inverse"], s["normed"], s["spread_normed"]
    before, activated, slope, grad_normed, grad_conv = s["before"], s["activated"], s["slope"], s["grad_normed"], s["grad_conv"]

    def row(vector):
        return vector[...].reshape(1, channels)

    def chunk(n):
        return pl.ds(pl.multiple_of(n * width, 128), width)

    def has_neighbour(side):
        return jnp.where(side == 0, strip > 0, strip < NROWS - 1)

    def halo_copy(strip_ref, halo, sems, side):
        first = pl.multiple_of(side * ((HROWS - REACH) * COLS), COLS)
        return send(strip_ref.at[pl.ds(first, REACH * COLS)], halo.at[1 - side], sems.at[0, side], sems.at[1, 1 - side],
                    peers.strip(2 * side - 1))

    def arrived(strip_ref, halo, sems, side):
        halo_copy(strip_ref, halo, sems, 1 - side).wait_recv()

    for rows in (source, gradient):
        rows[:REACH] = jnp.zeros((REACH, COLS, channels), F32)
        rows[REACH + HROWS :] = jnp.zeros((REACH, COLS, channels), F32)

    loads[0].wait()
    loads[1].wait()

    @pl.loop(0, HROWS)
    def _(h):
        at = pl.ds(pl.multiple_of(h * COLS, COLS), COLS)
        source[REACH + h] = images[at, :].astype(F32)
        scaled[at, :] = (cotangent[at, :].astype(F32) * row(scale)).astype(BF16)

    own_rows(source, conv, kernel, False)
    await_greetings(others)
    for side in (0, 1):

        @pl.when(has_neighbour(side))
        def _(side=side):
            halo_copy(images, s["image_halo"], s["image_sems"], side).start()

    spread_scaled[...] = spread_channels(scaled[...])
    loads[2].wait()

    @pl.loop(0, NZH)
    def _(n):
        grad_act[:, chunk(n)] = jnp.dot(scaled[...], down_weight[:, chunk(n)], preferred_element_type=F32)

    loads[3].wait()
    early = jnp.where((x == 0) & (c == 0), 1, 0)

    def part(rows, first, side, last):
        size = rows * COLS

        @pl.when(has_neighbour(side))
        def _():
            arrived(images, s["image_halo"], s["image_sems"], side)
            halo_rows(s["image_halo"], side, conv, kernel, False)

        pixels = pl.ds(pl.multiple_of(first * COLS, COLS), size)

        @pl.loop(0, rows)
        def _(k):
            h = first + k
            at = pl.ds(pl.multiple_of(h * COLS, COLS), COLS)
            value = conv[h] + row(conv_bias)
            centered = value - jnp.sum(value, axis=1, keepdims=True) * (1.0 / channels)
            inv = lax.rsqrt(jnp.sum(centered * centered, axis=1, keepdims=True) * (1.0 / channels) + EPSILON)
            std = centered * inv
            standard[at, :] = std
            inverse[at, :] = inv
            normed[at, :] = (std * row(gain) + row(shift)).astype(BF16)

        spread_normed[:size] = spread_channels(normed[pixels, :])

        @pl.loop(0, NZH)
        def _(n):
            weights = up_weight[:, chunk(n)]
            before[:size] = jnp.dot(normed[pixels, :], weights, preferred_element_type=F32)

            @pl.loop(0, size // TILE)
            def _(k):
                at = pl.ds(pl.multiple_of(k * TILE, TILE), TILE)
                act, slopes = gelu_parts(before[at, :] + up_bias[chunk(n)].reshape(1, width))
                activated[at, :] = act.astype(BF16)
                grads = grad_act[pl.ds(pl.multiple_of(first * COLS + k * TILE, TILE), TILE), chunk(n)]
                slope[at, :] = (grads * slopes).astype(BF16)

            sums.term(DOWN, n, activated[:size], spread_scaled[pixels, :], last)
            sums.term(UP, n, slope[:size], spread_normed[:size], last)
            back = lax.dot_general(slope[:size], weights, (((1,), (1,)), ((), ())), preferred_element_type=F32)

            @pl.when(n == 0)
            def _():
                grad_normed[:size] = back

            @pl.when(n > 0)
            def _():
                grad_normed[:size] = grad_normed[:size] + back

            if last:

                @pl.when(n > 0)
                def _():
                    sums.second(DOWN, n - 1)
                    sums.second(UP, n - 1)

        @pl.loop(0, rows)
        def _(k):
            h = first + k
            at = pl.ds(pl.multiple_of(h * COLS, COLS), COLS)
            gscaled = grad_normed[pl.ds(pl.multiple_of(k * COLS, COLS), COLS), :] * row(gain)
            std = standard[at, :]
            mean = jnp.sum(gscaled, axis=1, keepdims=True) * (1.0 / channels)
            along = jnp.sum(gscaled * std, axis=1, keepdims=True) * (1.0 / channels)
            value = (inverse[at, :] * (gscaled - mean - std * along)).astype(BF16)
            grad_conv[at, :] = value
            gradient[REACH + h] = value.astype(F32)

        @pl.when(has_neighbour(side))
        def _():
            halo_copy(grad_conv, s["grad_halo"], s["grad_sems"], side).start()

    part(PARTS[0], early * REACH, early, False)
    part(PARTS[1], (1 - early) * PARTS[0], 1 - early, True)
    for g in (DOWN, UP):
        sums.second(g, NZH - 1)
    own_rows(gradient, conv, kernel, True)
    for g in (DOWN, UP):
        sums.third(g)
    sums.fourth()
    sums.fifth()
    for step in (0, 1):
        side = jnp.where(step == 0, early, 1 - early)

        @pl.when(has_neighbour(side))
        def _(side=side):
            arrived(grad_conv, s["grad_halo"], s["grad_sems"], side)
            halo_rows(s["grad_halo"], side, conv, kernel, True)

    @pl.loop(0, HROWS)
    def _(h):
        at = pl.ds(pl.multiple_of(h * COLS, COLS), COLS)
        out[at, :] = (cotangent[at, :].astype(F32) + conv[h]).astype(BF16)

    store.start()
    sums.sixth()
    sums.finish(factor, up_out, down_out)
    sums.drain()
    store.wait()
    for strip_ref, halo, sems in ((images, s["image_halo"], s["image_sems"]), (grad_conv, s["grad_halo"], s["grad_sems"])):
        for side in (0, 1):

            @pl.when(has_neighbour(side))
            def _(strip_ref=strip_ref, halo=halo, sems=sems, side=side):
                halo_copy(strip_ref, halo, sems, side).wait_send()


TILE = 64


def hand_over(images, up, down, images_out, up_out, down_out, sem):
    copy = pltpu.make_async_copy(images, images_out, sem)
    copy.start()
    up_out[...] = up[...]
    down_out[...] = down[...]
    copy.wait()


def on_device(
    images,
    kernel,
    conv_bias,
    norm_gain,
    norm_shift,
    up_weight,
    up_bias,
    down_weight,
    layer_scale,
    cotangent,
):
    shape = images.shape
    channels, hidden = up_weight.shape
    pixels = shape[0] * shape[1] * shape[2]
    groups, parts = lax.axis_size("dp"), lax.axis_size("rows")
    factor = 1.0 / math.sqrt(pixels * groups * parts)
    scratch = reduce_scratch() | dict(
        source=pltpu.VMEM((HROWS + 2 * REACH, COLS, channels), F32),
        gradient=pltpu.VMEM((HROWS + 2 * REACH, COLS, channels), F32),
        conv=pltpu.VMEM((HROWS, COLS, channels), F32),
        up_weight=pltpu.VMEM(up_weight.shape, BF16),
        down_weight=pltpu.VMEM(down_weight.shape, BF16),
        images=pltpu.VMEM((pixels, channels), BF16),
        cotangent=pltpu.VMEM((pixels, channels), BF16),
        out=pltpu.VMEM((pixels, channels), BF16),
        load_sems=pltpu.SemaphoreType.DMA((5,)),
        scaled=pltpu.VMEM((pixels, channels), BF16),
        spread_scaled=pltpu.VMEM((pixels, NY * 128), BF16),
        grad_act=pltpu.VMEM((pixels, hidden), F32),
        standard=pltpu.VMEM((pixels, channels), F32),
        inverse=pltpu.VMEM((pixels, 1), F32),
        normed=pltpu.VMEM((pixels, channels), BF16),
        spread_normed=pltpu.VMEM((MOST, NY * 128), BF16),
        before=pltpu.VMEM((MOST, NX * NC * HB), F32),
        activated=pltpu.VMEM((MOST, NX * NC * HB), BF16),
        slope=pltpu.VMEM((MOST, NX * NC * HB), BF16),
        grad_normed=pltpu.VMEM((MOST, channels), F32),
        grad_conv=pltpu.VMEM((pixels, channels), BF16),
        image_halo=pltpu.VMEM((2, REACH * COLS, channels), BF16),
        grad_halo=pltpu.VMEM((2, REACH * COLS, channels), BF16),
        image_sems=pltpu.SemaphoreType.DMA((2, 2)),
        grad_sems=pltpu.SemaphoreType.DMA((2, 2)),
    )
    block = jax.ShapeDtypeStruct((CB, HB), F32)
    vmem, anywhere = pl.BlockSpec(memory_space=pltpu.VMEM), pl.BlockSpec(memory_space=pl.ANY)
    grad_images, grad_up, grad_down = pl.pallas_call(
        functools.partial(block_kernel, factor, tuple(scratch)),
        out_shape=(jax.ShapeDtypeStruct((pixels, channels), BF16), block, block),
        in_specs=[anywhere] + [vmem] * 4 + [anywhere, vmem, anywhere, vmem, anywhere],
        out_specs=(anywhere, vmem, vmem),
        scratch_shapes=list(scratch.values()),
        compiler_params=pltpu.CompilerParams(
            collective_id=0, has_side_effects=True, vmem_limit_bytes=56 * 1024 * 1024
        ),
    )(
        images.reshape(pixels, channels),
        kernel,
        conv_bias,
        norm_gain,
        norm_shift,
        up_weight,
        up_bias,
        down_weight,
        layer_scale,
        cotangent.reshape(pixels, channels),
    )
    grad_images, grad_up, grad_down = pl.pallas_call(
        hand_over,
        out_shape=(jax.ShapeDtypeStruct((pixels, channels), BF16), block, block),
        in_specs=[anywhere, vmem, vmem],
        out_specs=(anywhere, vmem, vmem),
        scratch_shapes=[pltpu.SemaphoreType.DMA],
    )(grad_images, grad_up, grad_down)
    return (grad_images.reshape(shape), grad_up, grad_down)


def solution(mesh):
    in_specs = (
        P("dp", "rows", None, None),
        P(),
        P(),
        P(),
        P(),
        P(),
        P(),
        P(),
        P(),
        P("dp", "rows", None, None),
    )
    out_specs = (P("dp", "rows", None, None), P("dp", "rows"), P("dp", "rows"))
    return jax.shard_map(
        on_device, mesh=mesh, in_specs=in_specs, out_specs=out_specs, check_vma=False
    )
```
